1024 devices in a mesh: space: 64 (over z, y_hi), src: 16 (over x, y_lo, core).
Axes of the slice: x: 4, y: 8 (y_hi: 4, y_lo: 2; y = y_hi * 2 + y_lo), z: 16, core: 2. Of those that a mesh axis runs over, the one named last changes fastest.
Arguments:
- misfit: float32 [128, 131072], P('src', 'space'), may hold values from -6 to 6
- electrode_node: int32 [131072], P('space'), may hold values from 0 to 2047
- forward_field: bfloat16 [128, 131072], P('src', 'space'), may hold values from -16 to 16
- diag_blocks: bfloat16 [64, 131072], P(None, 'space'), may hold values from -0.125 to 1.125
- precond: bfloat16 [64, 131072], P(None, 'space'), may hold values from -0.125 to 1.125
- off_blocks: bfloat16 [6, 64, 131072], P(None, None, 'space'), may hold values from -0.3125 to 0.3125
- off_index: int32 [2048, 6], P('space'), may hold values from 0 to 55, as said below
Outputs:
- adjoint: float32 [128, 131072], P('src', 'space')
- gradient: float32 [131072], P(('space', 'src'))
The draws below stay inside these ranges and needn't reach their ends.
Inputs may be any that keep to these rules, and one draw needn't show every extreme that they name: off_index of block b of a partition lies within b to b + 24 and is never b + 12.
All inputs are finite; a program needn't handle non-finite values.
Results may differ from the reference program's by a relative error of at most 0.0034.
Values may be sent and summed in bfloat16 or wider, within the bound.
A program may use at most 32 MiB of HBM per device.

```python
import jax
import jax.numpy as jnp
from jax import lax

NB = 32
B = 64
K = 6
SWEEPS = 3
ELEC = 2048
IB = 12
NBLK = 2048
NODES = 131072
SOURCES = 128
ELECS = 131072
N_SPACE = 64


def block_pair(key):
    base = jax.random.fold_in(key, 11)
    pert = jnp.clip(jax.random.normal(base, (NBLK, B, B), jnp.float32) * (0.25 / B ** 0.5), -0.125, 0.125)
    ident = jnp.eye(B, dtype=jnp.float32)[None]
    return (ident + pert, ident - pert)


def lay_out(blocks):
    return blocks.transpose(1, 0, 2).reshape(B, NBLK * B)


def draw_diag_blocks(key, part):
    return lay_out(block_pair(key)[0]).astype(jnp.bfloat16)


def draw_precond(key, part):
    return lay_out(block_pair(key)[1]).astype(jnp.bfloat16)


def draw_off_index(key, part):
    reach = jax.random.randint(jax.random.fold_in(key, 3), (NBLK, K), 1, IB + 1)
    sign = jax.random.randint(jax.random.fold_in(key, 5), (NBLK, K), 0, 2) * 2 - 1
    local = (jnp.arange(NBLK, dtype=jnp.int32) % NB)[:, None]
    column = jnp.arange(K, dtype=jnp.int32)[None, :]
    index = local + IB + sign * reach
    index = jnp.where((local == 0) & (column == 0), 0, index)
    index = jnp.where((local == NB - 1) & (column == 0), NB - 1 + 2 * IB, index)
    return index.astype(jnp.int32)


def set_ends(entries, own_key, low, top_value):
    extent = entries.shape
    spot = [jax.random.randint(jax.random.fold_in(own_key, axis), (), 0, extent[axis]) for axis in range(len(extent))]
    entries = entries.at[tuple(spot)].set(low)
    longest = extent.index(max(extent))
    spot[longest] = (spot[longest] + 1) % extent[longest]
    return entries.at[tuple(spot)].set(top_value)


def spiked(values, own_key, source, target, parts, factor):
    def block_of(axis_at):
        return (jnp.arange(values.shape[axis_at]) // (values.shape[axis_at] // parts)).reshape((-1,) + (1,) * (values.ndim - 1 - axis_at))

    one_side = jax.random.permutation(own_key, parts)[block_of(target)]
    other_side = (block_of(target) + parts // 2) % parts
    return jnp.where((block_of(source) == one_side) | (block_of(source) == other_side), factor * values, values)


def shard_levels(own_key, extent, shards, low, high):
    level, own = 1.0, jax.random.fold_in(own_key, 6)
    for dim, blocks in shards:
        heights = jnp.exp(jax.random.uniform(jax.random.fold_in(own, dim), (blocks,), jnp.float32, low / len(shards), high / len(shards)))
        level = level * jnp.repeat(heights, extent[dim] // blocks).reshape([-1 if axis == dim else 1 for axis in range(len(extent))])
    return level


def normal_values(rng, dims, spread, most, cuts=(), held_as=jnp.bfloat16):
    drawn = jax.random.normal(rng, dims, jnp.float32) * spread
    if len(cuts) > 0:
        drawn = shard_levels(rng, dims, cuts, -0.22, 0.18) * drawn
    return jnp.clip(drawn, min=-most, max=most).astype(held_as)


def gaussian_with(own_key, extent, deviation, most, shards, heavy, held_as=jnp.bfloat16):
    values = deviation * jax.random.normal(own_key, extent, jnp.float32)
    if shards:
        values = values * shard_levels(own_key, extent, shards, -0.22, 0.18)
    return jnp.clip(spiked(values, jax.random.fold_in(own_key, 3), *heavy), -most, most).astype(held_as)


def setup_inputs(seed: int = 0) -> dict:
    key_list = jax.random.split(jax.random.key(seed), 8)
    misfit = normal_values(key_list[0], (SOURCES, ELECS), 1.0, 6.0, ((0, 16), (1, 64)), jnp.float32)
    electrode_node = set_ends(jax.random.randint(key_list[1], (ELECS,), 0, NB * B), jax.random.fold_in(key_list[1], 1), 0, (NB * B) - 1).astype(jnp.int32)
    forward_field = gaussian_with(key_list[2], (SOURCES, NODES), 1.0, 16.0, ((0, 16), (1, 64)), (0, 1, 64, 4.0))
    diag_blocks = draw_diag_blocks(jax.random.fold_in(key_list[7], 71), 0)
    precond = draw_precond(jax.random.fold_in(key_list[7], 71), 0)
    off_blocks = normal_values(key_list[5], (K, B, NBLK * B), (0.4 / (B * K) ** 0.5), 0.3125, ((2, 64),))
    off_index = draw_off_index(jax.random.fold_in(key_list[7], 71), 0)
    return {"misfit": misfit, "electrode_node": electrode_node, "forward_field": forward_field, "diag_blocks": diag_blocks, "precond": precond, "off_blocks": off_blocks, "off_index": off_index}


def operate(field, diag_blocks, off_blocks, off_index):
    blocks = field.reshape(SOURCES, N_SPACE, NB, B)
    zero = jnp.zeros((SOURCES, 1, IB, B), field.dtype)
    lower = jnp.concatenate([zero, blocks[:, :-1, NB - IB:]], axis=1)
    upper = jnp.concatenate([blocks[:, 1:, :IB], zero], axis=1)
    extended = jnp.concatenate([lower, blocks, upper], axis=2).transpose(1, 0, 2, 3)
    diag_parts = diag_blocks.reshape(B, N_SPACE, NB, B).transpose(1, 2, 0, 3)
    off_parts = off_blocks.reshape(K, B, N_SPACE, NB, B).transpose(2, 3, 0, 1, 4)

    def one_part(item):
        ext_part, diag_part, off_part, index_part = item
        own = ext_part[:, IB:IB + NB]
        picked = ext_part[:, index_part]
        result = jnp.einsum('bij,sbj->sbi', diag_part.astype(jnp.float32), own.astype(jnp.float32))
        result = result + jnp.einsum('bkij,sbkj->sbi', off_part.astype(jnp.float32), picked.astype(jnp.float32))
        return result

    outcome = lax.map(one_part, (extended, diag_parts, off_parts,
                                 off_index.reshape(N_SPACE, NB, K)))
    return outcome.transpose(1, 0, 2, 3).reshape(SOURCES, NODES)


def smooth(residue, precond):
    rounded = residue.astype(jnp.bfloat16).reshape(SOURCES, NBLK, B)
    blocks = precond.reshape(B, NBLK, B)
    result = jnp.einsum('ibj,sbj->sbi', blocks.astype(jnp.float32), rounded.astype(jnp.float32))
    return result.reshape(SOURCES, NODES)


def reference(misfit, electrode_node, forward_field, diag_blocks, precond, off_blocks, off_index):
    owner = (jnp.arange(ELECS) // ELEC).astype(jnp.int32)
    global_node = (electrode_node + owner * (NB * B)).astype(jnp.int32)
    rhs = jnp.zeros((SOURCES, NODES), jnp.float32).at[:, global_node].add(misfit)
    lam = jnp.zeros((SOURCES, NODES), jnp.float32)
    for sweep in range(SWEEPS):
        if sweep == 0:
            residue = rhs
        else:
            residue = rhs - operate(lam.astype(jnp.bfloat16), diag_blocks, off_blocks, off_index)
        lam = lam + smooth(residue, precond)
    driven = operate(forward_field, diag_blocks, off_blocks, off_index)
    gradient = -jnp.sum(lam * driven, axis=0)
    return lam, gradient
```

```python
import functools

import jax
import jax.numpy as jnp
from jax import lax
from jax.experimental import pallas as pl
from jax.experimental.pallas import tpu as pltpu
from jax.sharding import PartitionSpec as P

MESH = pl.DeviceIdType.MESH
F32 = jnp.float32
BF16 = jnp.bfloat16
NT = (((1,), (1,)), ((), ()))


def kernel(
    cfg,
    misfit_h, node_h, field_h, diag_h, cond_h, off_h, index_h,
    lam_out, grad_out,
    misfit_v, node_v, field_v, diag_v, cond_v, off_v, index_s,
    rhs_v, lam_v, driven_v, tiles1, tiles2, tiles_f,
    stage, landed, grad_send, grad_recv,
    load_sem, halo_send, halo_recv, gsend_sem, grecv_sem,
):
    spaces, groups, pairs, rim, terms = cfg
    blocks = 2 * pairs
    ext = rim // 2
    inner = range(ext, pairs - ext)
    low = range(0, ext)
    high = range(pairs - ext, pairs)

    loads = []
    for at, (src, dst) in enumerate(
        [
            (node_h, node_v), (misfit_h, misfit_v), (cond_h, cond_v), (field_h, field_v),
            (index_h, index_s), (diag_h, diag_v), (off_h, off_v),
        ]
    ):
        copy = pltpu.make_async_copy(src, dst, load_sem.at[at])
        copy.start()
        loads.append(copy)
    node_l, misfit_l, cond_l, field_l, index_l, diag_l, off_l = loads

    me = lax.axis_index("space")
    group = lax.axis_index("src")
    down = lax.rem(me + spaces - 1, spaces)
    up = lax.rem(me + 1, spaces)
    barrier = pltpu.get_barrier_semaphore()
    for neighbour in (down, up):
        pl.semaphore_signal(barrier, inc=1, device_id={"space": neighbour}, device_id_type=MESH)
    for step in range(1, groups):
        peer = lax.rem(group + step, groups)
        pl.semaphore_signal(barrier, inc=1, device_id={"src": peer}, device_id_type=MESH)

    left = lax.broadcasted_iota(jnp.int32, (8, 128), 1) < 64
    upper_rows = lax.broadcasted_iota(jnp.int32, (16, 128), 0) < 8
    zero = jnp.zeros((8, 128), F32)

    def lanes(pair):
        return pl.ds(pair * 128, 128)

    node_l.wait()
    misfit_l.wait()
    chunk = 256
    total = None
    for at in range(0, misfit_v.shape[1], chunk):
        node = node_v[:, pl.ds(at, chunk)]
        pair_of = jnp.broadcast_to(node // 128, (8, chunk))
        lane_of = jnp.broadcast_to(node % 128, (128, chunk))
        value = misfit_v[:, pl.ds(at, chunk)]
        coarse = value.astype(BF16).astype(F32)
        fine = value - coarse
        rows = []
        for pair in range(pairs):
            mask = pair_of == pair
            rows.append(jnp.where(mask, coarse, 0.0))
            rows.append(jnp.where(mask, fine, 0.0))
        spread = jnp.concatenate(rows, axis=0).astype(BF16)
        hot = lax.broadcasted_iota(jnp.int32, (128, chunk), 0) == lane_of
        hot = jnp.where(hot, 1.0, 0.0).astype(BF16)
        part = lax.dot_general(spread, hot, NT, preferred_element_type=F32)
        total = part if total is None else total + part
    rhs = [total[16 * p : 16 * p + 8] + total[16 * p + 8 : 16 * p + 16] for p in range(pairs)]
    for pair in range(pairs):
        rhs_v[pair] = rhs[pair]

    def join(y):
        return jnp.where(left, y[0:8], y[8:16])

    def smooth(pair, res):
        x = jnp.concatenate([jnp.where(left, res, zero), jnp.where(left, zero, res)], axis=0)
        w = cond_v[:, lanes(pair)]
        w = jnp.concatenate([w, w], axis=0)
        return join(lax.dot_general(x.astype(BF16), w, NT, preferred_element_type=F32))

    def expand(tiles, first, v):
        swapped = pltpu.roll(v, 64, 1)
        tiles[first] = jnp.concatenate(
            [jnp.where(left, v, zero), jnp.where(left, zero, swapped)], axis=0
        ).astype(BF16)
        tiles[first + 1] = jnp.concatenate(
            [jnp.where(left, swapped, zero), jnp.where(left, zero, v)], axis=0
        ).astype(BF16)

    def apply(pair, tiles):
        parts = [jnp.where(upper_rows, tiles[rim + 2 * pair], tiles[rim + 2 * pair + 1])]
        weights = [diag_v[:, lanes(pair)]]
        for k in range(terms):
            parts.append(
                jnp.where(
                    upper_rows,
                    tiles[index_s[k, 2 * pair]],
                    tiles[index_s[k, 2 * pair + 1]],
                )
            )
            weights.append(off_v[k, :, lanes(pair)])
        x = jnp.concatenate(parts, axis=1)
        w = jnp.concatenate(weights, axis=1)
        w = jnp.concatenate([w, w], axis=0)
        return join(lax.dot_general(x, w, NT, preferred_element_type=F32))

    def stage_side(which, side, values):
        for at in range(0, ext, 2):
            stage[which, side, at // 2] = jnp.concatenate(
                [values[at], values[at + 1]], axis=0
            ).astype(BF16)

    def halo(which, side):
        return pltpu.make_async_remote_copy(
            src_ref=stage.at[which, side],
            dst_ref=landed.at[which, 1 - side],
            send_sem=halo_send.at[2 * which + side],
            recv_sem=halo_recv.at[2 * which + 1 - side],
            device_id={"space": down if side == 0 else up},
            device_id_type=MESH,
        )

    def receive(which, side, tiles):
        halo(which, 1 - side).wait_recv()
        have = me > 0 if side == 0 else me < spaces - 1
        base = 0 if side == 0 else rim + blocks
        for at in range(0, ext, 2):
            both = landed[which, side, at // 2].astype(F32)
            both = jnp.where(have, both, 0.0)
            expand(tiles, base + 2 * at, both[0:8])
            expand(tiles, base + 2 * at + 2, both[8:16])

    cond_l.wait()
    lam = [None] * pairs
    for pair in (*low, *high):
        lam[pair] = smooth(pair, rhs[pair])
    stage_side(0, 0, [lam[p] for p in low])
    stage_side(0, 1, [lam[p] for p in high])
    field_l.wait()
    field = [field_v[:, lanes(p)].astype(F32) for p in range(pairs)]
    stage_side(2, 0, [field[p] for p in low])
    stage_side(2, 1, [field[p] for p in high])

    pl.semaphore_wait(barrier, groups + 1)
    for which in (0, 2):
        for side in (0, 1):
            halo(which, side).start()

    for pair in inner:
        lam[pair] = smooth(pair, rhs[pair])
    for pair in range(pairs):
        lam_v[pair] = lam[pair]
        expand(tiles1, rim + 2 * pair, lam[pair])
        expand(tiles_f, rim + 2 * pair, field[pair])

    index_l.wait()
    diag_l.wait()
    off_l.wait()

    def sweep(pair, tiles):
        new = lam_v[pair] + smooth(pair, rhs_v[pair] - apply(pair, tiles))
        lam_v[pair] = new
        return new

    for pair in inner:
        lam[pair] = sweep(pair, tiles1)
    for side, own in ((0, low), (1, high)):
        receive(0, side, tiles1)
        for pair in own:
            lam[pair] = sweep(pair, tiles1)
        stage_side(1, side, [lam[p] for p in own])
        halo(1, side).start()
    for pair in range(pairs):
        expand(tiles2, rim + 2 * pair, lam[pair])

    for side in (0, 1):
        receive(2, side, tiles_f)
    for pair in range(pairs):
        driven_v[pair] = apply(pair, tiles_f)

    def send_row(pair):
        return pltpu.make_async_remote_copy(
            src_ref=grad_send.at[pair],
            dst_ref=grad_recv.at[group],
            send_sem=gsend_sem.at[pair],
            recv_sem=grecv_sem.at[group],
            device_id={"src": pair},
            device_id_type=MESH,
        )

    def finish(pair):
        new = sweep(pair, tiles2)
        lam_out[:, lanes(pair)] = new
        row = -jnp.sum(new * driven_v[pair], axis=0, keepdims=True)
        grad_send[pair] = row

        @pl.when(group != pair)
        def _():
            send_row(pair).start()

        @pl.when(group == pair)
        def _():
            grad_recv[pair] = row

    for pair in inner:
        finish(pair)
    for side, own in ((0, low), (1, high)):
        receive(1, side, tiles2)
        for pair in own:
            finish(pair)

    for which in range(3):
        for side in (0, 1):
            halo(which, side).wait_send()
    for peer in range(groups):

        @pl.when(group != peer)
        def _():
            pltpu.make_async_remote_copy(
                src_ref=grad_send.at[peer],
                dst_ref=grad_recv.at[peer],
                send_sem=gsend_sem.at[peer],
                recv_sem=grecv_sem.at[peer],
                device_id={"src": peer},
                device_id_type=MESH,
            ).wait()

    grad_out[...] = jnp.sum(grad_recv[...], axis=0)


def solution(mesh):
    spaces, groups = mesh.shape["space"], mesh.shape["src"]

    def shards(misfit, electrode_node, forward_field, diag_blocks, precond, off_blocks, off_index):
        sources, nodes = forward_field.shape
        width = diag_blocks.shape[0]
        blocks = nodes // width
        terms = off_blocks.shape[0]
        rim = 3 * blocks // 8
        pairs = blocks // 2
        electrodes = misfit.shape[1]
        ext_blocks = blocks + 2 * rim
        sent = rim // 4
        lam, grad = pl.pallas_call(
            functools.partial(kernel, (spaces, groups, pairs, rim, terms)),
            out_shape=(
                jax.ShapeDtypeStruct((sources, nodes), F32),
                jax.ShapeDtypeStruct((1, nodes // groups), F32),
            ),
            in_specs=[pl.BlockSpec(memory_space=pl.ANY)] * 7,
            out_specs=(pl.BlockSpec(memory_space=pltpu.VMEM), pl.BlockSpec(memory_space=pltpu.VMEM)),
            scratch_shapes=[
                pltpu.VMEM((sources, electrodes), F32),
                pltpu.VMEM((1, electrodes), jnp.int32),
                pltpu.VMEM((sources, nodes), BF16),
                pltpu.VMEM((width, nodes), BF16),
                pltpu.VMEM((width, nodes), BF16),
                pltpu.VMEM((terms, width, nodes), BF16),
                pltpu.SMEM((terms, blocks), jnp.int32),
                pltpu.VMEM((pairs, sources, 128), F32),
                pltpu.VMEM((pairs, sources, 128), F32),
                pltpu.VMEM((pairs, sources, 128), F32),
                pltpu.VMEM((ext_blocks, 16, 128), BF16),
                pltpu.VMEM((ext_blocks, 16, 128), BF16),
                pltpu.VMEM((ext_blocks, 16, 128), BF16),
                pltpu.VMEM((3, 2, sent, 16, 128), BF16),
                pltpu.VMEM((3, 2, sent, 16, 128), BF16),
                pltpu.VMEM((pairs, 1, 128), F32),
                pltpu.VMEM((groups, 1, 128), F32),
                pltpu.SemaphoreType.DMA((7,)),
                pltpu.SemaphoreType.DMA((6,)),
                pltpu.SemaphoreType.DMA((6,)),
                pltpu.SemaphoreType.DMA((pairs,)),
                pltpu.SemaphoreType.DMA((groups,)),
            ],
            compiler_params=pltpu.CompilerParams(
                collective_id=0, has_side_effects=True, vmem_limit_bytes=48 * 1024 * 1024
            ),
        )(
            misfit, electrode_node.reshape(1, electrodes), forward_field, diag_blocks, precond,
            off_blocks, off_index.T,
        )
        return lam, grad.reshape(nodes // groups)

    return jax.shard_map(
        shards,
        mesh=mesh,
        in_specs=(
            P("src", "space"),
            P("space"),
            P("src", "space"),
            P(None, "space"),
            P(None, "space"),
            P(None, None, "space"),
            P("space", None),
        ),
        out_specs=(P("src", "space"), P(("space", "src"))),
        check_vma=False,
    )
```

```python
import functools

import jax
import jax.numpy as jnp
from jax import lax
from jax.experimental import pallas as pl
from jax.experimental.pallas import tpu as pltpu
from jax.sharding import PartitionSpec as P

MESH = pl.DeviceIdType.MESH
F32 = jnp.float32
BF16 = jnp.bfloat16
NT = (((1,), (1,)), ((), ()))


def kernel(
    cfg,
    misfit_h, node_h, field_h, diag_h, cond_h, off_h, index_h,
    lam_out, grad_out,
    misfit_v, node_v, field_v, diag_v, cond_v, off_v, index_s,
    rhs_v, driven_v, tiles1, tiles2, tiles_f,
    stage, landed, grad_send, grad_recv,
    load_sem, halo_send, halo_recv, gsend_sem, grecv_sem,
):
    spaces, groups, pairs, rim, terms = cfg
    blocks = 2 * pairs
    ext = rim // 2
    inner = range(ext, pairs - ext)
    low = range(0, ext)
    high = range(pairs - ext, pairs)

    loads = []
    for at, (src, dst) in enumerate(
        [
            (node_h, node_v), (misfit_h, misfit_v), (cond_h, cond_v), (field_h, field_v),
            (index_h, index_s), (diag_h, diag_v), (off_h, off_v),
        ]
    ):
        copy = pltpu.make_async_copy(src, dst, load_sem.at[at])
        copy.start()
        loads.append(copy)
    node_l, misfit_l, cond_l, field_l, index_l, diag_l, off_l = loads

    me = lax.axis_index("space")
    group = lax.axis_index("src")
    down = lax.rem(me + spaces - 1, spaces)
    up = lax.rem(me + 1, spaces)
    barrier = pltpu.get_barrier_semaphore()
    for neighbour in (down, up):
        pl.semaphore_signal(barrier, inc=1, device_id={"space": neighbour}, device_id_type=MESH)
    for step in range(1, groups):
        peer = lax.rem(group + step, groups)
        pl.semaphore_signal(barrier, inc=1, device_id={"src": peer}, device_id_type=MESH)

    left = lax.broadcasted_iota(jnp.int32, (8, 128), 1) < 64
    upper_rows = lax.broadcasted_iota(jnp.int32, (16, 128), 0) < 8
    zero = jnp.zeros((8, 128), F32)

    def lanes(pair):
        return pl.ds(pair * 128, 128)

    node_l.wait()
    misfit_l.wait()
    chunk = 256
    total = None
    for at in range(0, misfit_v.shape[1], chunk):
        node = node_v[:, pl.ds(at, chunk)]
        pair_of = jnp.broadcast_to(node // 128, (8, chunk))
        lane_of = jnp.broadcast_to(node % 128, (128, chunk))
        value = misfit_v[:, pl.ds(at, chunk)]
        coarse = value.astype(BF16).astype(F32)
        fine = value - coarse
        rows = []
        for pair in range(pairs):
            mask = pair_of == pair
            rows.append(jnp.where(mask, coarse, 0.0))
            rows.append(jnp.where(mask, fine, 0.0))
        spread = jnp.concatenate(rows, axis=0).astype(BF16)
        hot = lax.broadcasted_iota(jnp.int32, (128, chunk), 0) == lane_of
        hot = jnp.where(hot, 1.0, 0.0).astype(BF16)
        part = lax.dot_general(spread, hot, NT, preferred_element_type=F32)
        total = part if total is None else total + part
    rhs = [total[16 * p : 16 * p + 8] + total[16 * p + 8 : 16 * p + 16] for p in range(pairs)]
    for pair in range(pairs):
        rhs_v[pair] = rhs[pair]

    def join(y):
        return jnp.where(left, y[0:8], y[8:16])

    def smooth(pair, res):
        x = jnp.concatenate([jnp.where(left, res, zero), jnp.where(left, zero, res)], axis=0)
        w = cond_v[:, lanes(pair)]
        w = jnp.concatenate([w, w], axis=0)
        return join(lax.dot_general(x.astype(BF16), w, NT, preferred_element_type=F32))

    def expand(tiles, first, v):
        swapped = pltpu.roll(v, 64, 1)
        tiles[first] = jnp.concatenate(
            [jnp.where(left, v, zero), jnp.where(left, zero, swapped)], axis=0
        ).astype(BF16)
        tiles[first + 1] = jnp.concatenate(
            [jnp.where(left, swapped, zero), jnp.where(left, zero, v)], axis=0
        ).astype(BF16)

    def apply(pair, tiles):
        parts = [jnp.where(upper_rows, tiles[rim + 2 * pair], tiles[rim + 2 * pair + 1])]
        weights = [diag_v[:, lanes(pair)]]
        for k in range(terms):
            parts.append(
                jnp.where(
                    upper_rows,
                    tiles[index_s[k, 2 * pair]],
                    tiles[index_s[k, 2 * pair + 1]],
                )
            )
            weights.append(off_v[k, :, lanes(pair)])
        x = jnp.concatenate(parts, axis=1)
        w = jnp.concatenate(weights, axis=1)
        w = jnp.concatenate([w, w], axis=0)
        return join(lax.dot_general(x, w, NT, preferred_element_type=F32))

    def stage_side(which, side, values):
        for at in range(0, ext, 2):
            stage[which, side, at // 2] = jnp.concatenate(
                [values[at], values[at + 1]], axis=0
            ).astype(BF16)

    def halo(which, side):
        return pltpu.make_async_remote_copy(
            src_ref=stage.at[which, side],
            dst_ref=landed.at[which, 1 - side],
            send_sem=halo_send.at[2 * which + side],
            recv_sem=halo_recv.at[2 * which + 1 - side],
            device_id={"space": down if side == 0 else up},
            device_id_type=MESH,
        )

    def receive(which, side, tiles):
        halo(which, 1 - side).wait_recv()
        have = me > 0 if side == 0 else me < spaces - 1
        base = 0 if side == 0 else rim + blocks
        for at in range(0, ext, 2):
            both = landed[which, side, at // 2].astype(F32)
            both = jnp.where(have, both, 0.0)
            expand(tiles, base + 2 * at, both[0:8])
            expand(tiles, base + 2 * at + 2, both[8:16])

    cond_l.wait()
    lam = [None] * pairs
    for pair in (*low, *high):
        lam[pair] = smooth(pair, rhs[pair])
    stage_side(0, 0, [lam[p] for p in low])
    stage_side(0, 1, [lam[p] for p in high])
    field_l.wait()
    field = [field_v[:, lanes(p)].astype(F32) for p in range(pairs)]
    stage_side(2, 0, [field[p] for p in low])
    stage_side(2, 1, [field[p] for p in high])

    pl.semaphore_wait(barrier, groups + 1)
    for which in (0, 2):
        for side in (0, 1):
            halo(which, side).start()

    for pair in inner:
        lam[pair] = smooth(pair, rhs[pair])
    for pair in range(pairs):
        expand(tiles1, rim + 2 * pair, lam[pair])
        expand(tiles_f, rim + 2 * pair, field[pair])

    index_l.wait()
    diag_l.wait()
    off_l.wait()

    def sweep(some, tiles):
        products = [apply(pair, tiles) for pair in some]
        steps = [smooth(pair, rhs_v[pair] - y) for pair, y in zip(some, products)]
        for pair, step in zip(some, steps):
            lam[pair] = lam[pair] + step

    sweep(inner, tiles1)
    for side, own in ((0, low), (1, high)):
        receive(0, side, tiles1)
        sweep(own, tiles1)
        stage_side(1, side, [lam[p] for p in own])
        halo(1, side).start()
    for pair in range(pairs):
        expand(tiles2, rim + 2 * pair, lam[pair])

    for side in (0, 1):
        receive(2, side, tiles_f)
    for pair in range(pairs):
        driven_v[pair] = apply(pair, tiles_f)

    def send_row(pair):
        return pltpu.make_async_remote_copy(
            src_ref=grad_send.at[pair],
            dst_ref=grad_recv.at[group],
            send_sem=gsend_sem.at[pair],
            recv_sem=grecv_sem.at[group],
            device_id={"src": pair},
            device_id_type=MESH,
        )

    def finish(some):
        sweep(some, tiles2)
        rows = [-jnp.sum(lam[p] * driven_v[p], axis=0, keepdims=True) for p in some]
        for pair, row in zip(some, rows):
            grad_send[pair] = row
            lam_out[:, lanes(pair)] = lam[pair]
        for pair in some:

            @pl.when(group != pair)
            def _():
                send_row(pair).start()

    finish(inner)
    for side, own in ((0, low), (1, high)):
        receive(1, side, tiles2)
        finish(own)

    grad_recv[pl.ds(group, 1)] = grad_send[pl.ds(group, 1)]
    for which in range(3):
        for side in (0, 1):
            halo(which, side).wait_send()
    for peer in range(groups):

        @pl.when(group != peer)
        def _():
            pltpu.make_async_remote_copy(
                src_ref=grad_send.at[peer],
                dst_ref=grad_recv.at[peer],
                send_sem=gsend_sem.at[peer],
                recv_sem=grecv_sem.at[peer],
                device_id={"src": peer},
                device_id_type=MESH,
            ).wait()

    grad_out[...] = jnp.sum(grad_recv[...], axis=0)


def solution(mesh):
    spaces, groups = mesh.shape["space"], mesh.shape["src"]

    def shards(misfit, electrode_node, forward_field, diag_blocks, precond, off_blocks, off_index):
        sources, nodes = forward_field.shape
        width = diag_blocks.shape[0]
        blocks = nodes // width
        terms = off_blocks.shape[0]
        rim = 3 * blocks // 8
        pairs = blocks // 2
        electrodes = misfit.shape[1]
        ext_blocks = blocks + 2 * rim
        sent = rim // 4
        lam, grad = pl.pallas_call(
            functools.partial(kernel, (spaces, groups, pairs, rim, terms)),
            out_shape=(
                jax.ShapeDtypeStruct((sources, nodes), F32),
                jax.ShapeDtypeStruct((1, nodes // groups), F32),
            ),
            in_specs=[pl.BlockSpec(memory_space=pltpu.HBM)] * 7,
            out_specs=(pl.BlockSpec(memory_space=pltpu.VMEM), pl.BlockSpec(memory_space=pltpu.VMEM)),
            scratch_shapes=[
                pltpu.VMEM((sources, electrodes), F32),
                pltpu.VMEM((1, electrodes), jnp.int32),
                pltpu.VMEM((sources, nodes), BF16),
                pltpu.VMEM((width, nodes), BF16),
                pltpu.VMEM((width, nodes), BF16),
                pltpu.VMEM((terms, width, nodes), BF16),
                pltpu.SMEM((terms, blocks), jnp.int32),
                pltpu.VMEM((pairs, sources, 128), F32),
                pltpu.VMEM((pairs, sources, 128), F32),
                pltpu.VMEM((ext_blocks, 16, 128), BF16),
                pltpu.VMEM((ext_blocks, 16, 128), BF16),
                pltpu.VMEM((ext_blocks, 16, 128), BF16),
                pltpu.VMEM((3, 2, sent, 16, 128), BF16),
                pltpu.VMEM((3, 2, sent, 16, 128), BF16),
                pltpu.VMEM((pairs, 1, 128), F32),
                pltpu.VMEM((groups, 1, 128), F32),
                pltpu.SemaphoreType.DMA((7,)),
                pltpu.SemaphoreType.DMA((6,)),
                pltpu.SemaphoreType.DMA((6,)),
                pltpu.SemaphoreType.DMA((pairs,)),
                pltpu.SemaphoreType.DMA((groups,)),
            ],
            compiler_params=pltpu.CompilerParams(
                collective_id=0, has_side_effects=True, vmem_limit_bytes=60 * 1024 * 1024
            ),
        )(
            misfit, electrode_node.reshape(1, electrodes), forward_field, diag_blocks, precond,
            off_blocks, off_index.T,
        )
        return lam, grad.reshape(nodes // groups)

    return jax.shard_map(
        shards,
        mesh=mesh,
        in_specs=(
            P("src", "space"),
            P("space"),
            P("src", "space"),
            P(None, "space"),
            P(None, "space"),
            P(None, None, "space"),
            P("space", None),
        ),
        out_specs=(P("src", "space"), P(("space", "src"))),
        check_vma=False,
    )
```

```python
import functools

import jax
import jax.numpy as jnp
from jax import lax
from jax.experimental import pallas as pl
from jax.experimental.pallas import tpu as pltpu
from jax.sharding import PartitionSpec as P

MESH = pl.DeviceIdType.MESH
F32 = jnp.float32
BF16 = jnp.bfloat16
NT = (((1,), (1,)), ((), ()))


def kernel(
    cfg,
    misfit_h, node_h, field_h, diag_h, cond_h, off_h, index_h,
    lam_out, grad_out,
    misfit_v, node_v, field_v, diag_v, cond_v, off_v, index_s,
    rhs_v, driven_v, tiles1, tiles2, tiles_f,
    stage, landed, grad_send, grad_recv,
    load_sem, halo_send, halo_recv, gsend_sem, grecv_sem,
):
    spaces, groups, pairs, rim, terms = cfg
    blocks = 2 * pairs
    ext = rim // 2
    inner = range(ext, pairs - ext)
    low = range(0, ext)
    high = range(pairs - ext, pairs)

    loads = []
    for at, (src, dst) in enumerate(
        [
            (node_h, node_v), (misfit_h, misfit_v), (cond_h, cond_v), (field_h, field_v),
            (index_h, index_s), (diag_h, diag_v), (off_h, off_v),
        ]
    ):
        copy = pltpu.make_async_copy(src, dst, load_sem.at[at])
        copy.start()
        loads.append(copy)
    node_l, misfit_l, cond_l, field_l, index_l, diag_l, off_l = loads

    me = lax.axis_index("space")
    group = lax.axis_index("src")
    down = lax.rem(me + spaces - 1, spaces)
    up = lax.rem(me + 1, spaces)
    barrier = pltpu.get_barrier_semaphore()
    has = (me > 0, me < spaces - 1)
    for side, neighbour in enumerate((down, up)):

        @pl.when(has[side])
        def _():
            pl.semaphore_signal(
                barrier, inc=1, device_id={"space": neighbour}, device_id_type=MESH
            )

    for step in range(1, groups):
        peer = lax.rem(group + step, groups)
        pl.semaphore_signal(barrier, inc=1, device_id={"src": peer}, device_id_type=MESH)

    left = lax.broadcasted_iota(jnp.int32, (8, 128), 1) < 64
    upper_rows = lax.broadcasted_iota(jnp.int32, (16, 128), 0) < 8
    zero = jnp.zeros((8, 128), F32)

    def lanes(pair):
        return pl.ds(pair * 128, 128)

    node_l.wait()
    misfit_l.wait()
    chunk = 256
    total = None
    for at in range(0, misfit_v.shape[1], chunk):
        node = node_v[:, pl.ds(at, chunk)]
        pair_of = jnp.broadcast_to(node // 128, (8, chunk))
        lane_of = jnp.broadcast_to(node % 128, (128, chunk))
        value = misfit_v[:, pl.ds(at, chunk)]
        coarse = value.astype(BF16).astype(F32)
        fine = value - coarse
        rows = []
        for pair in range(pairs):
            mask = pair_of == pair
            rows.append(jnp.where(mask, coarse, 0.0))
            rows.append(jnp.where(mask, fine, 0.0))
        spread = jnp.concatenate(rows, axis=0).astype(BF16)
        hot = lax.broadcasted_iota(jnp.int32, (128, chunk), 0) == lane_of
        hot = jnp.where(hot, 1.0, 0.0).astype(BF16)
        part = lax.dot_general(spread, hot, NT, preferred_element_type=F32)
        total = part if total is None else total + part
    rhs = [total[16 * p : 16 * p + 8] + total[16 * p + 8 : 16 * p + 16] for p in range(pairs)]
    for pair in range(pairs):
        rhs_v[pair] = rhs[pair]

    def join(y):
        return jnp.concatenate([y[0:8], y[8:16]], axis=1)

    def smooth(pair, res):
        x = jnp.concatenate([jnp.where(left, res, zero), jnp.where(left, zero, res)], axis=0)
        w = cond_v[:, lanes(pair)]
        return join(lax.dot_general(x.astype(BF16), w, NT, preferred_element_type=F32))

    def expand(tiles, first, v):
        swapped = pltpu.roll(v, 64, 1)
        tiles[first] = jnp.concatenate(
            [jnp.where(left, v, zero), jnp.where(left, zero, swapped)], axis=0
        ).astype(BF16)
        tiles[first + 1] = jnp.concatenate(
            [jnp.where(left, swapped, zero), jnp.where(left, zero, v)], axis=0
        ).astype(BF16)

    def apply(pair, tiles):
        parts = [jnp.where(upper_rows, tiles[rim + 2 * pair], tiles[rim + 2 * pair + 1])]
        weights = [diag_v[:, lanes(pair)]]
        for k in range(terms):
            parts.append(
                jnp.where(
                    upper_rows,
                    tiles[index_s[k, 2 * pair]],
                    tiles[index_s[k, 2 * pair + 1]],
                )
            )
            weights.append(off_v[k, :, lanes(pair)])
        x = jnp.concatenate(parts, axis=1)
        w = jnp.concatenate(weights, axis=1)
        return join(lax.dot_general(x, w, NT, preferred_element_type=F32))

    def stage_side(which, side, values):
        for at in range(0, ext, 2):
            stage[which, side, at // 2] = jnp.concatenate(
                [values[at], values[at + 1]], axis=0
            ).astype(BF16)

    def halo(which, side):
        return pltpu.make_async_remote_copy(
            src_ref=stage.at[which, side],
            dst_ref=landed.at[which, 1 - side],
            send_sem=halo_send.at[2 * which + side],
            recv_sem=halo_recv.at[2 * which + 1 - side],
            device_id={"space": down if side == 0 else up},
            device_id_type=MESH,
        )

    def start(which, side):
        @pl.when(has[side])
        def _():
            halo(which, side).start()

    def receive(which, side, tiles):
        @pl.when(has[side])
        def _():
            halo(which, 1 - side).wait_recv()

        base = 0 if side == 0 else rim + blocks
        for at in range(0, ext, 2):
            both = landed[which, side, at // 2].astype(F32)
            both = jnp.where(has[side], both, 0.0)
            expand(tiles, base + 2 * at, both[0:8])
            expand(tiles, base + 2 * at + 2, both[8:16])

    cond_l.wait()
    lam = [None] * pairs
    for pair in (*low, *high):
        lam[pair] = smooth(pair, rhs[pair])
    stage_side(0, 0, [lam[p] for p in low])
    stage_side(0, 1, [lam[p] for p in high])
    field_l.wait()
    field = [field_v[:, lanes(p)].astype(F32) for p in range(pairs)]
    stage_side(2, 0, [field[p] for p in low])
    stage_side(2, 1, [field[p] for p in high])

    pl.semaphore_wait(
        barrier, groups - 1 + jnp.where(has[0], 1, 0) + jnp.where(has[1], 1, 0)
    )
    for which in (0, 2):
        for side in (0, 1):
            start(which, side)

    for pair in inner:
        lam[pair] = smooth(pair, rhs[pair])
    for pair in range(pairs):
        expand(tiles1, rim + 2 * pair, lam[pair])
        expand(tiles_f, rim + 2 * pair, field[pair])

    index_l.wait()
    diag_l.wait()
    off_l.wait()

    def sweep(some, tiles):
        products = [apply(pair, tiles) for pair in some]
        steps = [smooth(pair, rhs_v[pair] - y) for pair, y in zip(some, products)]
        for pair, step in zip(some, steps):
            lam[pair] = lam[pair] + step

    sweep(inner, tiles1)
    for side, own in ((0, low), (1, high)):
        receive(0, side, tiles1)
        sweep(own, tiles1)
        stage_side(1, side, [lam[p] for p in own])
        start(1, side)
    for pair in range(pairs):
        expand(tiles2, rim + 2 * pair, lam[pair])

    for side in (0, 1):
        receive(2, side, tiles_f)
    for pair in range(pairs):
        driven_v[pair] = apply(pair, tiles_f)

    def send_row(pair):
        return pltpu.make_async_remote_copy(
            src_ref=grad_send.at[pair],
            dst_ref=grad_recv.at[group],
            send_sem=gsend_sem.at[pair],
            recv_sem=grecv_sem.at[group],
            device_id={"src": pair},
            device_id_type=MESH,
        )

    def finish(some):
        sweep(some, tiles2)
        rows = [-jnp.sum(lam[p] * driven_v[p], axis=0, keepdims=True) for p in some]
        for pair, row in zip(some, rows):
            grad_send[pair] = row
            lam_out[:, lanes(pair)] = lam[pair]
        for pair in some:

            @pl.when(group != pair)
            def _():
                send_row(pair).start()

    finish(inner)
    for side, own in ((0, low), (1, high)):
        receive(1, side, tiles2)
        finish(own)

    grad_recv[pl.ds(group, 1)] = grad_send[pl.ds(group, 1)]
    for which in range(3):
        for side in (0, 1):

            @pl.when(has[side])
            def _():
                halo(which, side).wait_send()

    for peer in range(groups):

        @pl.when(group != peer)
        def _():
            pltpu.make_async_remote_copy(
                src_ref=grad_send.at[peer],
                dst_ref=grad_recv.at[peer],
                send_sem=gsend_sem.at[peer],
                recv_sem=grecv_sem.at[peer],
                device_id={"src": peer},
                device_id_type=MESH,
            ).wait()

    grad_out[...] = jnp.sum(grad_recv[...], axis=0)


def write_out(lam, grad, lam_out, grad_out, sem):
    copies = [
        pltpu.make_async_copy(lam, lam_out, sem.at[0]),
        pltpu.make_async_copy(grad, grad_out, sem.at[1]),
    ]
    for copy in copies:
        copy.start()
    for copy in copies:
        copy.wait()


def solution(mesh):
    spaces, groups = mesh.shape["space"], mesh.shape["src"]

    def shards(misfit, electrode_node, forward_field, diag_blocks, precond, off_blocks, off_index):
        sources, nodes = forward_field.shape
        width = diag_blocks.shape[0]
        blocks = nodes // width
        terms = off_blocks.shape[0]
        rim = 3 * blocks // 8
        pairs = blocks // 2
        electrodes = misfit.shape[1]
        ext_blocks = blocks + 2 * rim
        sent = rim // 4
        lam, grad = pl.pallas_call(
            functools.partial(kernel, (spaces, groups, pairs, rim, terms)),
            out_shape=(
                pltpu.VMEM((sources, nodes), F32),
                pltpu.VMEM((1, nodes // groups), F32),
            ),
            in_specs=[pl.BlockSpec(memory_space=pltpu.HBM)] * 7,
            out_specs=(pl.BlockSpec(memory_space=pltpu.VMEM), pl.BlockSpec(memory_space=pltpu.VMEM)),
            scratch_shapes=[
                pltpu.VMEM((sources, electrodes), F32),
                pltpu.VMEM((1, electrodes), jnp.int32),
                pltpu.VMEM((sources, nodes), BF16),
                pltpu.VMEM((width, nodes), BF16),
                pltpu.VMEM((width, nodes), BF16),
                pltpu.VMEM((terms, width, nodes), BF16),
                pltpu.SMEM((terms, blocks), jnp.int32),
                pltpu.VMEM((pairs, sources, 128), F32),
                pltpu.VMEM((pairs, sources, 128), F32),
                pltpu.VMEM((ext_blocks, 16, 128), BF16),
                pltpu.VMEM((ext_blocks, 16, 128), BF16),
                pltpu.VMEM((ext_blocks, 16, 128), BF16),
                pltpu.VMEM((3, 2, sent, 16, 128), BF16),
                pltpu.VMEM((3, 2, sent, 16, 128), BF16),
                pltpu.VMEM((pairs, 1, 128), F32),
                pltpu.VMEM((groups, 1, 128), F32),
                pltpu.SemaphoreType.DMA((7,)),
                pltpu.SemaphoreType.DMA((6,)),
                pltpu.SemaphoreType.DMA((6,)),
                pltpu.SemaphoreType.DMA((pairs,)),
                pltpu.SemaphoreType.DMA((groups,)),
            ],
            compiler_params=pltpu.CompilerParams(
                collective_id=0, has_side_effects=True, vmem_limit_bytes=32 * 1024 * 1024
            ),
        )(
            *(
                pltpu.with_memory_space_constraint(operand, pltpu.HBM)
                for operand in (
                    misfit, electrode_node.reshape(1, electrodes), forward_field, diag_blocks,
                    precond, off_blocks, off_index.T,
                )
            )
        )
        lam, grad = pl.pallas_call(
            write_out,
            out_shape=(
                pltpu.HBM((sources, nodes), F32),
                pltpu.HBM((1, nodes // groups), F32),
            ),
            in_specs=[pl.BlockSpec(memory_space=pltpu.VMEM)] * 2,
            out_specs=(pl.BlockSpec(memory_space=pltpu.HBM),) * 2,
            scratch_shapes=[pltpu.SemaphoreType.DMA((2,))],
        )(
            pltpu.with_memory_space_constraint(lam, pltpu.VMEM),
            pltpu.with_memory_space_constraint(grad, pltpu.VMEM),
        )
        return lam, grad.reshape(nodes // groups)

    return jax.shard_map(
        shards,
        mesh=mesh,
        in_specs=(
            P("src", "space"),
            P("space"),
            P("src", "space"),
            P(None, "space"),
            P(None, "space"),
            P(None, None, "space"),
            P("space", None),
        ),
        out_specs=(P("src", "space"), P(("space", "src"))),
        check_vma=False,
    )
```

```python
import functools

import jax
import jax.numpy as jnp
from jax import lax
from jax.experimental import pallas as pl
from jax.experimental.pallas import tpu as pltpu
from jax.sharding import PartitionSpec as P

MESH = pl.DeviceIdType.MESH
F32 = jnp.float32
BF16 = jnp.bfloat16
NT = (((1,), (1,)), ((), ()))


def kernel(
    cfg,
    misfit_h, node_h, field_h, diag_h, cond_h, off_h, index_h,
    lam_out, grad_out,
    misfit_v, node_v, field_v, diag_v, cond_v, off_v, index_s,
    rhs_v, driven_v, tiles1, tiles2, tiles_f,
    stage, landed, grad_send, grad_recv,
    load_sem, halo_send, halo_recv, gsend_sem, grecv_sem, present,
):
    spaces, groups, pairs, rim, terms = cfg
    blocks = 2 * pairs
    ext = rim // 2
    inner = range(ext, pairs - ext)
    low = range(0, ext)
    high = range(pairs - ext, pairs)

    loads = []
    for at, (src, dst) in enumerate(
        [
            (misfit_h, misfit_v), (node_h, node_v), (cond_h, cond_v), (field_h, field_v),
            (index_h, index_s), (diag_h, diag_v), (off_h, off_v),
        ]
    ):
        loads.append(pltpu.make_async_copy(src, dst, load_sem.at[at]))
    misfit_l, node_l, cond_l, field_l, index_l, diag_l, off_l = loads
    for copy in loads[:3]:
        copy.start()

    me = lax.axis_index("space")
    group = lax.axis_index("src")
    down = lax.rem(me + spaces - 1, spaces)
    up = lax.rem(me + 1, spaces)
    barrier = pltpu.get_barrier_semaphore()
    has = (me > 0, me < spaces - 1)
    for side, neighbour in enumerate((down, up)):

        @pl.when(has[side])
        def _():
            pl.semaphore_signal(
                barrier, inc=1, device_id={"space": neighbour}, device_id_type=MESH
            )

    core = group + 1 - 2 * lax.rem(group, 2)
    across = group + 2 - 4 * lax.rem(lax.div(group, 2), 2)
    after = lax.rem(group + 4, groups)
    before = lax.rem(group + groups - 4, groups)
    for peer in (after, before, across, core):
        pl.semaphore_signal(barrier, inc=1, device_id={"src": peer}, device_id_type=MESH)
    for copy in loads[3:]:
        copy.start()

    left = lax.broadcasted_iota(jnp.int32, (8, 128), 1) < 64
    upper_rows = lax.broadcasted_iota(jnp.int32, (16, 128), 0) < 8
    zero = jnp.zeros((8, 128), F32)

    def lanes(pair):
        return pl.ds(pair * 128, 128)

    node_l.wait()
    misfit_l.wait()
    chunk = 256
    total = None
    for at in range(0, misfit_v.shape[1], chunk):
        node = node_v[:, pl.ds(at, chunk)]
        pair_of = jnp.broadcast_to(node // 128, (8, chunk))
        lane_of = jnp.broadcast_to(node % 128, (128, chunk))
        value = misfit_v[:, pl.ds(at, chunk)]
        coarse = value.astype(BF16).astype(F32)
        fine = value - coarse
        rows = []
        for pair in range(pairs):
            mask = pair_of == pair
            rows.append(jnp.where(mask, coarse, 0.0))
            rows.append(jnp.where(mask, fine, 0.0))
        spread = jnp.concatenate(rows, axis=0).astype(BF16)
        hot = lax.broadcasted_iota(jnp.int32, (128, chunk), 0) == lane_of
        hot = jnp.where(hot, 1.0, 0.0).astype(BF16)
        part = lax.dot_general(spread, hot, NT, preferred_element_type=F32)
        total = part if total is None else total + part
    rhs = [total[16 * p : 16 * p + 8] + total[16 * p + 8 : 16 * p + 16] for p in range(pairs)]
    for pair in range(pairs):
        rhs_v[pair] = rhs[pair]

    def join(y):
        return jnp.concatenate([y[0:8], y[8:16]], axis=1)

    def smooth(pair, res):
        x = jnp.concatenate([jnp.where(left, res, zero), jnp.where(left, zero, res)], axis=0)
        w = cond_v[:, lanes(pair)]
        return join(lax.dot_general(x.astype(BF16), w, NT, preferred_element_type=F32))

    def expand(tiles, first, v):
        swapped = pltpu.roll(v, 64, 1)
        tiles[first] = jnp.concatenate(
            [jnp.where(left, v, zero), jnp.where(left, zero, swapped)], axis=0
        ).astype(BF16)
        tiles[first + 1] = jnp.concatenate(
            [jnp.where(left, swapped, zero), jnp.where(left, zero, v)], axis=0
        ).astype(BF16)

    def apply(pair, tiles):
        parts = [jnp.where(upper_rows, tiles[rim + 2 * pair], tiles[rim + 2 * pair + 1])]
        weights = [diag_v[:, lanes(pair)]]
        for k in range(terms):
            parts.append(
                jnp.where(
                    upper_rows,
                    tiles[index_s[k, 2 * pair]],
                    tiles[index_s[k, 2 * pair + 1]],
                )
            )
            weights.append(off_v[k, :, lanes(pair)])
        x = jnp.concatenate(parts, axis=1)
        w = jnp.concatenate(weights, axis=1)
        return join(lax.dot_general(x, w, NT, preferred_element_type=F32))

    def stage_side(which, side, values):
        for at in range(0, ext, 2):
            stage[side, which, at // 2] = jnp.concatenate(
                [values[at], values[at + 1]], axis=0
            ).astype(BF16)

    def halo(which, side):
        return pltpu.make_async_remote_copy(
            src_ref=stage.at[side, which],
            dst_ref=landed.at[which, 1 - side],
            send_sem=halo_send.at[side],
            recv_sem=halo_recv.at[2 * which + 1 - side],
            device_id={"space": down if side == 0 else up},
            device_id_type=MESH,
        )

    def start(which, side):
        @pl.when(has[side])
        def _():
            halo(which, side).start()

    def receive(which, side, tiles):
        @pl.when(has[side])
        def _():
            halo(which, 1 - side).wait_recv()

        base = 0 if side == 0 else rim + blocks
        for at in range(0, ext, 2):
            both = landed[which, side, at // 2].astype(F32)
            both = jnp.where(has[side], both, 0.0)
            expand(tiles, base + 2 * at, both[0:8])
            expand(tiles, base + 2 * at + 2, both[8:16])

    cond_l.wait()
    lam = [None] * pairs
    for pair in (*high, *low):
        lam[pair] = smooth(pair, rhs[pair])
    stage_side(0, 1, [lam[p] for p in high])
    stage_side(0, 0, [lam[p] for p in low])
    pl.semaphore_wait(
        barrier, 4 + jnp.where(has[0], 1, 0) + jnp.where(has[1], 1, 0)
    )
    for side in (1, 0):
        start(0, side)
    field_l.wait()
    field = [field_v[:, lanes(p)].astype(F32) for p in range(pairs)]
    for side, own in ((1, high), (0, low)):
        stage_side(2, side, [field[p] for p in own])
        start(2, side)

    def tell(at, peer):
        pl.semaphore_signal(
            present.at[at], inc=1, device_id={"src": peer}, device_id_type=MESH
        )

    tell(0, after)
    for pair in inner:
        lam[pair] = smooth(pair, rhs[pair])
    for pair in range(pairs):
        expand(tiles1, rim + 2 * pair, lam[pair])
        expand(tiles_f, rim + 2 * pair, field[pair])

    index_l.wait()
    diag_l.wait()
    off_l.wait()

    def sweep(some, tiles):
        products = [apply(pair, tiles) for pair in some]
        steps = [smooth(pair, rhs_v[pair] - y) for pair, y in zip(some, products)]
        for pair, step in zip(some, steps):
            lam[pair] = lam[pair] + step

    sweep(inner, tiles1)
    for side, own in ((1, high), (0, low)):
        receive(0, side, tiles1)
        sweep(own, tiles1)
        stage_side(1, side, [lam[p] for p in own])
        start(1, side)
    pl.semaphore_wait(present.at[0], 1)
    tell(1, across)
    for pair in range(pairs):
        expand(tiles2, rim + 2 * pair, lam[pair])

    for side in (1, 0):
        receive(2, side, tiles_f)
    for pair in range(pairs):
        driven_v[pair] = apply(pair, tiles_f)

    pl.semaphore_wait(present.at[1], 1)
    tell(2, core)

    def send_row(pair):
        return pltpu.make_async_remote_copy(
            src_ref=grad_send.at[pair],
            dst_ref=grad_recv.at[group],
            send_sem=gsend_sem.at[0],
            recv_sem=grecv_sem.at[0],
            device_id={"src": pair},
            device_id_type=MESH,
        )

    def finish(some):
        sweep(some, tiles2)
        rows = [-jnp.sum(lam[p] * driven_v[p], axis=0, keepdims=True) for p in some]
        for pair, row in zip(some, rows):
            grad_send[pair] = row
            lam_out[:, lanes(pair)] = lam[pair]
        for pair in some:

            @pl.when(group != pair)
            def _():
                send_row(pair).start()

    pl.semaphore_wait(present.at[2], 1)
    finish(inner)
    for side, own in ((0, low), (1, high)):
        receive(1, side, tiles2)
        finish(own)

    grad_recv[pl.ds(group, 1)] = grad_send[pl.ds(group, 1)]
    for side in (0, 1):

        @pl.when(has[side])
        def _():
            pltpu.make_async_copy(stage.at[side], stage.at[side], halo_send.at[side]).wait()

    others = pl.ds(0, groups - 1)
    for sem in (gsend_sem, grecv_sem):
        pltpu.make_async_copy(grad_send.at[others], grad_recv.at[others], sem.at[0]).wait()

    grad_out[...] = jnp.sum(grad_recv[...], axis=0)


def write_out(lam, grad, lam_out, grad_out, sem):
    copies = [
        pltpu.make_async_copy(lam, lam_out, sem.at[0]),
        pltpu.make_async_copy(grad, grad_out, sem.at[1]),
    ]
    for copy in copies:
        copy.start()
    for copy in copies:
        copy.wait()


def solution(mesh):
    spaces, groups = mesh.shape["space"], mesh.shape["src"]

    def shards(misfit, electrode_node, forward_field, diag_blocks, precond, off_blocks, off_index):
        sources, nodes = forward_field.shape
        width = diag_blocks.shape[0]
        blocks = nodes // width
        terms = off_blocks.shape[0]
        rim = 3 * blocks // 8
        pairs = blocks // 2
        electrodes = misfit.shape[1]
        ext_blocks = blocks + 2 * rim
        sent = rim // 4
        lam, grad = pl.pallas_call(
            functools.partial(kernel, (spaces, groups, pairs, rim, terms)),
            out_shape=(
                pltpu.VMEM((sources, nodes), F32),
                pltpu.VMEM((1, nodes // groups), F32),
            ),
            in_specs=[pl.BlockSpec(memory_space=pltpu.HBM)] * 7,
            out_specs=(pl.BlockSpec(memory_space=pltpu.VMEM), pl.BlockSpec(memory_space=pltpu.VMEM)),
            scratch_shapes=[
                pltpu.VMEM((sources, electrodes), F32),
                pltpu.VMEM((1, electrodes), jnp.int32),
                pltpu.VMEM((sources, nodes), BF16),
                pltpu.VMEM((width, nodes), BF16),
                pltpu.VMEM((width, nodes), BF16),
                pltpu.VMEM((terms, width, nodes), BF16),
                pltpu.SMEM((terms, blocks), jnp.int32),
                pltpu.VMEM((pairs, sources, 128), F32),
                pltpu.VMEM((pairs, sources, 128), F32),
                pltpu.VMEM((ext_blocks, 16, 128), BF16),
                pltpu.VMEM((ext_blocks, 16, 128), BF16),
                pltpu.VMEM((ext_blocks, 16, 128), BF16),
                pltpu.VMEM((2, 3, sent, 16, 128), BF16),
                pltpu.VMEM((3, 2, sent, 16, 128), BF16),
                pltpu.VMEM((pairs, 1, 128), F32),
                pltpu.VMEM((groups, 1, 128), F32),
                pltpu.SemaphoreType.DMA((7,)),
                pltpu.SemaphoreType.DMA((2,)),
                pltpu.SemaphoreType.DMA((6,)),
                pltpu.SemaphoreType.DMA((1,)),
                pltpu.SemaphoreType.DMA((1,)),
                pltpu.SemaphoreType.REGULAR((3,)),
            ],
            compiler_params=pltpu.CompilerParams(
                collective_id=0, has_side_effects=True, vmem_limit_bytes=32 * 1024 * 1024
            ),
        )(
            *(
                pltpu.with_memory_space_constraint(operand, pltpu.HBM)
                for operand in (
                    misfit, electrode_node.reshape(1, electrodes), forward_field, diag_blocks,
                    precond, off_blocks, off_index.T,
                )
            )
        )
        lam, grad = pl.pallas_call(
            write_out,
            out_shape=(
                pltpu.HBM((sources, nodes), F32),
                pltpu.HBM((1, nodes // groups), F32),
            ),
            in_specs=[pl.BlockSpec(memory_space=pltpu.VMEM)] * 2,
            out_specs=(pl.BlockSpec(memory_space=pltpu.HBM),) * 2,
            scratch_shapes=[pltpu.SemaphoreType.DMA((2,))],
        )(
            pltpu.with_memory_space_constraint(lam, pltpu.VMEM),
            pltpu.with_memory_space_constraint(grad, pltpu.VMEM),
        )
        return lam, grad.reshape(nodes // groups)

    return jax.shard_map(
        shards,
        mesh=mesh,
        in_specs=(
            P("src", "space"),
            P("space"),
            P("src", "space"),
            P(None, "space"),
            P(None, "space"),
            P(None, None, "space"),
            P("space", None),
        ),
        out_specs=(P("src", "space"), P(("space", "src"))),
        check_vma=False,
    )
```

```python
import functools

import jax
import jax.numpy as jnp
from jax import lax
from jax.experimental import pallas as pl
from jax.experimental.pallas import tpu as pltpu
from jax.sharding import PartitionSpec as P

MESH = pl.DeviceIdType.MESH
F32 = jnp.float32
BF16 = jnp.bfloat16
NT = (((1,), (1,)), ((), ()))


def kernel(
    cfg,
    misfit_h, node_h, field_h, diag_h, cond_h, off_h, index_h,
    lam_out, grad_out,
    misfit_v, node_v, field_v, diag_v, cond_v, off_v, index_s,
    rhs_v, cond2_v, driven_v, tiles1, tiles2, tiles_f,
    stage, landed, grad_send, grad_recv,
    load_sem, halo_send, halo_recv, gsend_sem, grecv_sem, present,
):
    spaces, groups, pairs, rim, terms = cfg
    blocks = 2 * pairs
    ext = rim // 2
    inner = range(ext, pairs - ext)
    low = range(0, ext)
    high = range(pairs - ext, pairs)

    loads = []
    for at, (src, dst) in enumerate(
        [
            (misfit_h, misfit_v), (node_h, node_v), (cond_h, cond_v), (field_h, field_v),
            (index_h, index_s), (diag_h, diag_v), (off_h, off_v),
        ]
    ):
        loads.append(pltpu.make_async_copy(src, dst, load_sem.at[at]))
    misfit_l, node_l, cond_l, field_l, index_l, diag_l, off_l = loads
    for copy in loads[:3]:
        copy.start()

    me = lax.axis_index("space")
    group = lax.axis_index("src")
    down = lax.rem(me + spaces - 1, spaces)
    up = lax.rem(me + 1, spaces)
    barrier = pltpu.get_barrier_semaphore()
    has = (me > 0, me < spaces - 1)
    for side, neighbour in enumerate((down, up)):

        @pl.when(has[side])
        def _():
            pl.semaphore_signal(
                barrier, inc=1, device_id={"space": neighbour}, device_id_type=MESH
            )

    core = group + 1 - 2 * lax.rem(group, 2)
    across = group + 2 - 4 * lax.rem(lax.div(group, 2), 2)
    after = lax.rem(group + 4, groups)
    before = lax.rem(group + groups - 4, groups)
    for peer in (after, before, across, core):
        pl.semaphore_signal(barrier, inc=1, device_id={"src": peer}, device_id_type=MESH)
    for copy in loads[3:]:
        copy.start()

    left = lax.broadcasted_iota(jnp.int32, (8, 128), 1) < 64
    upper_rows = lax.broadcasted_iota(jnp.int32, (16, 128), 0) < 8
    zero = jnp.zeros((8, 128), F32)

    def lanes(pair):
        return pl.ds(pair * 128, 128)

    node_l.wait()
    misfit_l.wait()
    chunk = 256
    total = None
    for at in range(0, misfit_v.shape[1], chunk):
        node = node_v[:, pl.ds(at, chunk)]
        pair_of = jnp.broadcast_to(node // 128, (8, chunk))
        lane_of = jnp.broadcast_to(node % 128, (128, chunk))
        value = misfit_v[:, pl.ds(at, chunk)]
        coarse = value.astype(BF16).astype(F32)
        fine = value - coarse
        rows = []
        for pair in range(pairs):
            mask = pair_of == pair
            rows.append(jnp.where(mask, coarse, 0.0))
            rows.append(jnp.where(mask, fine, 0.0))
        spread = jnp.concatenate(rows, axis=0).astype(BF16)
        hot = lax.broadcasted_iota(jnp.int32, (128, chunk), 0) == lane_of
        hot = jnp.where(hot, 1.0, 0.0).astype(BF16)
        part = lax.dot_general(spread, hot, NT, preferred_element_type=F32)
        total = part if total is None else total + part
    rhs = [total[16 * p : 16 * p + 8] + total[16 * p + 8 : 16 * p + 16] for p in range(pairs)]

    def pick(y):
        return jnp.where(left, y[0:8], y[8:16])

    def smooth(pair, res):
        x = jnp.concatenate([jnp.where(left, res, zero), jnp.where(left, zero, res)], axis=0)
        w = cond_v[:, lanes(pair)]
        w = jnp.concatenate([w, w], axis=0)
        return pick(lax.dot_general(x.astype(BF16), w, NT, preferred_element_type=F32))

    def expand(tiles, first, v):
        swapped = pltpu.roll(v, 64, 1)
        tiles[first] = jnp.concatenate(
            [jnp.where(left, v, zero), jnp.where(left, zero, swapped)], axis=0
        ).astype(BF16)
        tiles[first + 1] = jnp.concatenate(
            [jnp.where(left, swapped, zero), jnp.where(left, zero, v)], axis=0
        ).astype(BF16)

    def apply(pair, tiles):
        parts = [jnp.where(upper_rows, tiles[rim + 2 * pair], tiles[rim + 2 * pair + 1])]
        weights = [diag_v[:, lanes(pair)]]
        for k in range(terms):
            parts.append(
                jnp.where(
                    upper_rows,
                    tiles[index_s[k, 2 * pair]],
                    tiles[index_s[k, 2 * pair + 1]],
                )
            )
            weights.append(off_v[k, :, lanes(pair)])
        x = jnp.concatenate(parts, axis=1)
        w = jnp.concatenate(weights, axis=1)
        return lax.dot_general(x, w, NT, preferred_element_type=F32)

    def stage_side(which, side, values):
        for at in range(0, ext, 2):
            stage[side, which, at // 2] = jnp.concatenate(
                [values[at], values[at + 1]], axis=0
            ).astype(BF16)

    def halo(which, side):
        return pltpu.make_async_remote_copy(
            src_ref=stage.at[side, which],
            dst_ref=landed.at[which, 1 - side],
            send_sem=halo_send.at[side],
            recv_sem=halo_recv.at[2 * which + 1 - side],
            device_id={"space": down if side == 0 else up},
            device_id_type=MESH,
        )

    def start(which, side):
        @pl.when(has[side])
        def _():
            halo(which, side).start()

    def receive(which, side, tiles):
        @pl.when(has[side])
        def _():
            halo(which, 1 - side).wait_recv()

        base = 0 if side == 0 else rim + blocks
        for at in range(0, ext, 2):
            both = landed[which, side, at // 2].astype(F32)
            both = jnp.where(has[side], both, 0.0)
            expand(tiles, base + 2 * at, both[0:8])
            expand(tiles, base + 2 * at + 2, both[8:16])

    cond_l.wait()
    lam = [None] * pairs
    for pair in high:
        lam[pair] = smooth(pair, rhs[pair])
    stage_side(0, 1, [lam[p] for p in high])
    pl.semaphore_wait(barrier, 4 + jnp.where(has[0], 1, 0) + jnp.where(has[1], 1, 0))
    start(0, 1)
    for pair in low:
        lam[pair] = smooth(pair, rhs[pair])
    stage_side(0, 0, [lam[p] for p in low])
    start(0, 0)
    field_l.wait()
    field = [field_v[:, lanes(p)].astype(F32) for p in range(pairs)]
    for side, own in ((1, high), (0, low)):
        stage_side(2, side, [field[p] for p in own])
        start(2, side)

    def tell(at, peer):
        pl.semaphore_signal(
            present.at[at], inc=1, device_id={"src": peer}, device_id_type=MESH
        )

    tell(0, after)
    for pair in inner:
        lam[pair] = smooth(pair, rhs[pair])
    for pair in range(pairs):
        expand(tiles1, rim + 2 * pair, lam[pair])
        expand(tiles_f, rim + 2 * pair, field[pair])

    for pair in range(pairs):
        rhs_v[pair] = jnp.concatenate([rhs[pair], pltpu.roll(rhs[pair], 64, 1)], axis=0)
        w = cond_v[:, lanes(pair)]
        cond2_v[pair] = jnp.concatenate([w[:, 0:64], w[:, 64:128]], axis=0)

    index_l.wait()
    diag_l.wait()
    off_l.wait()

    def sweep(some, tiles):
        products = [apply(pair, tiles) for pair in some]
        residues = [
            (rhs_v[pair, :, 0:64] - y).astype(BF16) for pair, y in zip(some, products)
        ]
        steps = [
            lax.dot_general(res, cond2_v[pair], NT, preferred_element_type=F32)
            for pair, res in zip(some, residues)
        ]
        for pair, step in zip(some, steps):
            lam[pair] = lam[pair] + pick(step)

    pl.semaphore_wait(present.at[0], 1)
    tell(1, across)
    sweep(inner, tiles1)
    pl.semaphore_wait(present.at[1], 1)
    tell(2, core)
    for side, own in ((1, high), (0, low)):
        receive(0, side, tiles1)
        sweep(own, tiles1)
        stage_side(1, side, [lam[p] for p in own])
        start(1, side)
    for pair in range(pairs):
        expand(tiles2, rim + 2 * pair, lam[pair])

    for side in (1, 0):
        receive(2, side, tiles_f)
    for pair in range(pairs):
        y = apply(pair, tiles_f)
        driven_v[pair] = jnp.concatenate([y[0:8], y[8:16]], axis=1)

    def send_row(pair):
        return pltpu.make_async_remote_copy(
            src_ref=grad_send.at[pair],
            dst_ref=grad_recv.at[group],
            send_sem=gsend_sem.at[0],
            recv_sem=grecv_sem.at[0],
            device_id={"src": pair},
            device_id_type=MESH,
        )

    def finish(some):
        sweep(some, tiles2)
        rows = [-jnp.sum(lam[p] * driven_v[p], axis=0, keepdims=True) for p in some]
        for pair, row in zip(some, rows):
            grad_send[pair] = row
            lam_out[:, lanes(pair)] = lam[pair]
        for pair in some:

            @pl.when(group != pair)
            def _():
                send_row(pair).start()

    pl.semaphore_wait(present.at[2], 1)
    finish(inner)
    for side, own in ((0, low), (1, high)):
        receive(1, side, tiles2)
        finish(own)

    grad_recv[pl.ds(group, 1)] = grad_send[pl.ds(group, 1)]
    for side in (0, 1):

        @pl.when(has[side])
        def _():
            pltpu.make_async_copy(stage.at[side], stage.at[side], halo_send.at[side]).wait()

    others = pl.ds(0, groups - 1)
    for sem in (gsend_sem, grecv_sem):
        pltpu.make_async_copy(grad_send.at[others], grad_recv.at[others], sem.at[0]).wait()

    grad_out[...] = jnp.sum(grad_recv[...], axis=0)


def write_out(lam, grad, lam_out, grad_out, sem):
    copies = [
        pltpu.make_async_copy(lam, lam_out, sem.at[0]),
        pltpu.make_async_copy(grad, grad_out, sem.at[1]),
    ]
    for copy in copies:
        copy.start()
    for copy in copies:
        copy.wait()


def solution(mesh):
    spaces, groups = mesh.shape["space"], mesh.shape["src"]

    def shards(misfit, electrode_node, forward_field, diag_blocks, precond, off_blocks, off_index):
        sources, nodes = forward_field.shape
        width = diag_blocks.shape[0]
        blocks = nodes // width
        terms = off_blocks.shape[0]
        rim = 3 * blocks // 8
        pairs = blocks // 2
        electrodes = misfit.shape[1]
        ext_blocks = blocks + 2 * rim
        sent = rim // 4
        lam, grad = pl.pallas_call(
            functools.partial(kernel, (spaces, groups, pairs, rim, terms)),
            out_shape=(
                pltpu.VMEM((sources, nodes), F32),
                pltpu.VMEM((1, nodes // groups), F32),
            ),
            in_specs=[pl.BlockSpec(memory_space=pltpu.HBM)] * 7,
            out_specs=(pl.BlockSpec(memory_space=pltpu.VMEM), pl.BlockSpec(memory_space=pltpu.VMEM)),
            scratch_shapes=[
                pltpu.VMEM((sources, electrodes), F32),
                pltpu.VMEM((1, electrodes), jnp.int32),
                pltpu.VMEM((sources, nodes), BF16),
                pltpu.VMEM((width, nodes), BF16),
                pltpu.VMEM((width, nodes), BF16),
                pltpu.VMEM((terms, width, nodes), BF16),
                pltpu.SMEM((terms, blocks), jnp.int32),
                pltpu.VMEM((pairs, 16, 128), F32),
                pltpu.VMEM((pairs, 128, width), BF16),
                pltpu.VMEM((pairs, sources, 128), F32),
                pltpu.VMEM((ext_blocks, 16, 128), BF16),
                pltpu.VMEM((ext_blocks, 16, 128), BF16),
                pltpu.VMEM((ext_blocks, 16, 128), BF16),
                pltpu.VMEM((2, 3, sent, 16, 128), BF16),
                pltpu.VMEM((3, 2, sent, 16, 128), BF16),
                pltpu.VMEM((pairs, 1, 128), F32),
                pltpu.VMEM((groups, 1, 128), F32),
                pltpu.SemaphoreType.DMA((7,)),
                pltpu.SemaphoreType.DMA((2,)),
                pltpu.SemaphoreType.DMA((6,)),
                pltpu.SemaphoreType.DMA((1,)),
                pltpu.SemaphoreType.DMA((1,)),
                pltpu.SemaphoreType.REGULAR((3,)),
            ],
            compiler_params=pltpu.CompilerParams(
                collective_id=0, has_side_effects=True, vmem_limit_bytes=32 * 1024 * 1024
            ),
        )(
            *(
                pltpu.with_memory_space_constraint(operand, pltpu.HBM)
                for operand in (
                    misfit, electrode_node.reshape(1, electrodes), forward_field, diag_blocks,
                    precond, off_blocks, off_index.T,
                )
            )
        )
        lam, grad = pl.pallas_call(
            write_out,
            out_shape=(
                pltpu.HBM((sources, nodes), F32),
                pltpu.HBM((1, nodes // groups), F32),
            ),
            in_specs=[pl.BlockSpec(memory_space=pltpu.VMEM)] * 2,
            out_specs=(pl.BlockSpec(memory_space=pltpu.HBM),) * 2,
            scratch_shapes=[pltpu.SemaphoreType.DMA((2,))],
        )(
            pltpu.with_memory_space_constraint(lam, pltpu.VMEM),
            pltpu.with_memory_space_constraint(grad, pltpu.VMEM),
        )
        return lam, grad.reshape(nodes // groups)

    return jax.shard_map(
        shards,
        mesh=mesh,
        in_specs=(
            P("src", "space"),
            P("space"),
            P("src", "space"),
            P(None, "space"),
            P(None, "space"),
            P(None, None, "space"),
            P("space", None),
        ),
        out_specs=(P("src", "space"), P(("space", "src"))),
        check_vma=False,
    )
```

```python
import functools

import jax
import jax.numpy as jnp
from jax import lax
from jax.experimental import pallas as pl
from jax.experimental.pallas import tpu as pltpu
from jax.sharding import PartitionSpec as P

MESH = pl.DeviceIdType.MESH
F32 = jnp.float32
BF16 = jnp.bfloat16
NT = (((1,), (1,)), ((), ()))


def kernel(
    cfg,
    misfit_h, node_h, field_h, diag_h, cond_h, off_h, index_h,
    lam_out, grad_out,
    misfit_v, node_v, field_v, diag_v, cond_v, off_v, index_s,
    rhs_v, cond2_v, driven_v, tiles1, tiles2, tiles_f,
    stage, landed, grad_send, grad_recv,
    load_sem, halo_send, halo_recv, gsend_sem, grecv_sem, present,
):
    spaces, groups, pairs, rim, terms = cfg
    blocks = 2 * pairs
    ext = rim // 2
    inner = range(ext, pairs - ext)
    low = range(0, ext)
    high = range(pairs - ext, pairs)

    loads = []
    for at, (src, dst) in enumerate(
        [
            (misfit_h, misfit_v), (node_h, node_v), (cond_h, cond_v), (field_h, field_v),
            (index_h, index_s), (diag_h, diag_v), (off_h, off_v),
        ]
    ):
        loads.append(pltpu.make_async_copy(src, dst, load_sem.at[at]))
    misfit_l, node_l, cond_l, field_l, index_l, diag_l, off_l = loads

    me = lax.axis_index("space")
    group = lax.axis_index("src")
    down = lax.rem(me + spaces - 1, spaces)
    up = lax.rem(me + 1, spaces)
    barrier = pltpu.get_barrier_semaphore()
    has = (me > 0, me < spaces - 1)
    for side, neighbour in enumerate((down, up)):

        @pl.when(has[side])
        def _():
            pl.semaphore_signal(
                barrier, inc=1, device_id={"space": neighbour}, device_id_type=MESH
            )

    core = group + 1 - 2 * lax.rem(group, 2)
    across = group + 2 - 4 * lax.rem(lax.div(group, 2), 2)
    after = lax.rem(group + 4, groups)
    before = lax.rem(group + groups - 4, groups)
    for peer in (after, before, across, core):
        pl.semaphore_signal(barrier, inc=1, device_id={"src": peer}, device_id_type=MESH)
    for copy in loads:
        copy.start()

    left = lax.broadcasted_iota(jnp.int32, (8, 128), 1) < 64
    upper_rows = lax.broadcasted_iota(jnp.int32, (16, 128), 0) < 8
    zero = jnp.zeros((8, 128), F32)

    def lanes(pair):
        return pl.ds(pair * 128, 128)

    node_l.wait()
    misfit_l.wait()
    chunk = 256
    total = None
    for at in range(0, misfit_v.shape[1], chunk):
        node = node_v[:, pl.ds(at, chunk)]
        pair_of = jnp.broadcast_to(node // 128, (8, chunk))
        lane_of = jnp.broadcast_to(node % 128, (128, chunk))
        value = misfit_v[:, pl.ds(at, chunk)]
        coarse = value.astype(BF16).astype(F32)
        fine = value - coarse
        rows = []
        for pair in range(pairs):
            mask = pair_of == pair
            rows.append(jnp.where(mask, coarse, 0.0))
            rows.append(jnp.where(mask, fine, 0.0))
        spread = jnp.concatenate(rows, axis=0).astype(BF16)
        hot = lax.broadcasted_iota(jnp.int32, (128, chunk), 0) == lane_of
        hot = jnp.where(hot, 1.0, 0.0).astype(BF16)
        part = lax.dot_general(spread, hot, NT, preferred_element_type=F32)
        total = part if total is None else total + part
    rhs = [total[16 * p : 16 * p + 8] + total[16 * p + 8 : 16 * p + 16] for p in range(pairs)]

    def pick(y):
        return jnp.where(left, y[0:8], y[8:16])

    def smooth(pair, res):
        x = jnp.concatenate([jnp.where(left, res, zero), jnp.where(left, zero, res)], axis=0)
        w = cond_v[:, lanes(pair)]
        w = jnp.concatenate([w, w], axis=0)
        return pick(lax.dot_general(x.astype(BF16), w, NT, preferred_element_type=F32))

    def expand(tiles, first, v):
        swapped = pltpu.roll(v, 64, 1)
        tiles[first] = jnp.concatenate(
            [jnp.where(left, v, zero), jnp.where(left, zero, swapped)], axis=0
        ).astype(BF16)
        tiles[first + 1] = jnp.concatenate(
            [jnp.where(left, swapped, zero), jnp.where(left, zero, v)], axis=0
        ).astype(BF16)

    def apply(pair, tiles):
        parts = [jnp.where(upper_rows, tiles[rim + 2 * pair], tiles[rim + 2 * pair + 1])]
        weights = [diag_v[:, lanes(pair)]]
        for k in range(terms):
            parts.append(
                jnp.where(
                    upper_rows,
                    tiles[index_s[k, 2 * pair]],
                    tiles[index_s[k, 2 * pair + 1]],
                )
            )
            weights.append(off_v[k, :, lanes(pair)])
        x = jnp.concatenate(parts, axis=1)
        w = jnp.concatenate(weights, axis=1)
        return lax.dot_general(x, w, NT, preferred_element_type=F32)

    def stage_side(which, side, values):
        for at in range(0, ext, 2):
            stage[side, which, at // 2] = jnp.concatenate(
                [values[at], values[at + 1]], axis=0
            ).astype(BF16)

    def halo(which, side):
        return pltpu.make_async_remote_copy(
            src_ref=stage.at[side, which],
            dst_ref=landed.at[which, 1 - side],
            send_sem=halo_send.at[side],
            recv_sem=halo_recv.at[2 * which + 1 - side],
            device_id={"space": down if side == 0 else up},
            device_id_type=MESH,
        )

    def start(which, side):
        @pl.when(has[side])
        def _():
            halo(which, side).start()

    def receive(which, side, tiles):
        @pl.when(has[side])
        def _():
            halo(which, 1 - side).wait_recv()

        base = 0 if side == 0 else rim + blocks
        for at in range(0, ext, 2):
            both = landed[which, side, at // 2].astype(F32)
            both = jnp.where(has[side], both, 0.0)
            expand(tiles, base + 2 * at, both[0:8])
            expand(tiles, base + 2 * at + 2, both[8:16])

    cond_l.wait()
    lam = [None] * pairs
    for pair in high:
        lam[pair] = smooth(pair, rhs[pair])
    stage_side(0, 1, [lam[p] for p in high])
    pl.semaphore_wait(barrier, 4 + jnp.where(has[0], 1, 0) + jnp.where(has[1], 1, 0))
    start(0, 1)
    def tell(at, peer):
        pl.semaphore_signal(
            present.at[at], inc=1, device_id={"src": peer}, device_id_type=MESH
        )

    tell(0, after)
    for pair in low:
        lam[pair] = smooth(pair, rhs[pair])
    stage_side(0, 0, [lam[p] for p in low])
    start(0, 0)
    field_l.wait()
    field = [field_v[:, lanes(p)].astype(F32) for p in range(pairs)]
    for side, own in ((1, high), (0, low)):
        stage_side(2, side, [field[p] for p in own])
        start(2, side)

    for pair in inner:
        lam[pair] = smooth(pair, rhs[pair])
    for pair in range(pairs):
        expand(tiles1, rim + 2 * pair, lam[pair])
        expand(tiles_f, rim + 2 * pair, field[pair])

    for pair in range(pairs):
        rhs_v[pair] = jnp.concatenate([rhs[pair], pltpu.roll(rhs[pair], 64, 1)], axis=0)
        w = cond_v[:, lanes(pair)]
        cond2_v[pair] = jnp.concatenate([w[:, 0:64], w[:, 64:128]], axis=0)

    index_l.wait()
    diag_l.wait()
    off_l.wait()

    def sweep(some, tiles):
        products = [apply(pair, tiles) for pair in some]
        residues = [
            (rhs_v[pair, :, 0:64] - y).astype(BF16) for pair, y in zip(some, products)
        ]
        steps = [
            lax.dot_general(res, cond2_v[pair], NT, preferred_element_type=F32)
            for pair, res in zip(some, residues)
        ]
        for pair, step in zip(some, steps):
            lam[pair] = lam[pair] + pick(step)

    pl.semaphore_wait(present.at[0], 1)
    tell(1, across)
    sweep(inner, tiles1)
    pl.semaphore_wait(present.at[1], 1)
    tell(2, core)
    for side, own in ((1, high), (0, low)):
        receive(0, side, tiles1)
        sweep(own, tiles1)
        stage_side(1, side, [lam[p] for p in own])
        start(1, side)
    for pair in range(pairs):
        expand(tiles2, rim + 2 * pair, lam[pair])

    for side in (1, 0):
        receive(2, side, tiles_f)
    for pair in range(pairs):
        y = apply(pair, tiles_f)
        driven_v[pair] = jnp.concatenate([y[0:8], y[8:16]], axis=1)

    def send_row(pair):
        return pltpu.make_async_remote_copy(
            src_ref=grad_send.at[pair],
            dst_ref=grad_recv.at[group],
            send_sem=gsend_sem.at[0],
            recv_sem=grecv_sem.at[0],
            device_id={"src": pair},
            device_id_type=MESH,
        )

    def finish(some, first=False):
        sweep(some, tiles2)
        rows = [-jnp.sum(lam[p] * driven_v[p], axis=0, keepdims=True) for p in some]
        for pair, row in zip(some, rows):
            grad_send[pair] = row
            lam_out[:, lanes(pair)] = lam[pair]
        if first:
            pl.semaphore_wait(present.at[2], 1)
        for pair in some:

            @pl.when(group != pair)
            def _():
                send_row(pair).start()

    finish(inner, first=True)
    for side, own in ((0, low), (1, high)):
        receive(1, side, tiles2)
        finish(own)

    grad_recv[pl.ds(group, 1)] = grad_send[pl.ds(group, 1)]
    for side in (0, 1):

        @pl.when(has[side])
        def _():
            pltpu.make_async_copy(stage.at[side], stage.at[side], halo_send.at[side]).wait()

    others = pl.ds(0, groups - 1)
    for sem in (gsend_sem, grecv_sem):
        pltpu.make_async_copy(grad_send.at[others], grad_recv.at[others], sem.at[0]).wait()

    grad_out[...] = jnp.sum(grad_recv[...], axis=0)


def write_out(lam, grad, lam_out, grad_out, sem):
    copies = [
        pltpu.make_async_copy(lam, lam_out, sem.at[0]),
        pltpu.make_async_copy(grad, grad_out, sem.at[1]),
    ]
    for copy in copies:
        copy.start()
    for copy in copies:
        copy.wait()


def solution(mesh):
    spaces, groups = mesh.shape["space"], mesh.shape["src"]

    def shards(misfit, electrode_node, forward_field, diag_blocks, precond, off_blocks, off_index):
        sources, nodes = forward_field.shape
        width = diag_blocks.shape[0]
        blocks = nodes // width
        terms = off_blocks.shape[0]
        rim = 3 * blocks // 8
        pairs = blocks // 2
        electrodes = misfit.shape[1]
        ext_blocks = blocks + 2 * rim
        sent = rim // 4
        lam, grad = pl.pallas_call(
            functools.partial(kernel, (spaces, groups, pairs, rim, terms)),
            out_shape=(
                pltpu.VMEM((sources, nodes), F32),
                pltpu.VMEM((1, nodes // groups), F32),
            ),
            in_specs=[pl.BlockSpec(memory_space=pltpu.HBM)] * 7,
            out_specs=(pl.BlockSpec(memory_space=pltpu.VMEM), pl.BlockSpec(memory_space=pltpu.VMEM)),
            scratch_shapes=[
                pltpu.VMEM((sources, electrodes), F32),
                pltpu.VMEM((1, electrodes), jnp.int32),
                pltpu.VMEM((sources, nodes), BF16),
                pltpu.VMEM((width, nodes), BF16),
                pltpu.VMEM((width, nodes), BF16),
                pltpu.VMEM((terms, width, nodes), BF16),
                pltpu.SMEM((terms, blocks), jnp.int32),
                pltpu.VMEM((pairs, 16, 128), F32),
                pltpu.VMEM((pairs, 128, width), BF16),
                pltpu.VMEM((pairs, sources, 128), F32),
                pltpu.VMEM((ext_blocks, 16, 128), BF16),
                pltpu.VMEM((ext_blocks, 16, 128), BF16),
                pltpu.VMEM((ext_blocks, 16, 128), BF16),
                pltpu.VMEM((2, 3, sent, 16, 128), BF16),
                pltpu.VMEM((3, 2, sent, 16, 128), BF16),
                pltpu.VMEM((pairs, 1, 128), F32),
                pltpu.VMEM((groups, 1, 128), F32),
                pltpu.SemaphoreType.DMA((7,)),
                pltpu.SemaphoreType.DMA((2,)),
                pltpu.SemaphoreType.DMA((6,)),
                pltpu.SemaphoreType.DMA((1,)),
                pltpu.SemaphoreType.DMA((1,)),
                pltpu.SemaphoreType.REGULAR((3,)),
            ],
            compiler_params=pltpu.CompilerParams(
                collective_id=0, has_side_effects=True, vmem_limit_bytes=32 * 1024 * 1024
            ),
        )(
            *(
                pltpu.with_memory_space_constraint(operand, pltpu.HBM)
                for operand in (
                    misfit, electrode_node.reshape(1, electrodes), forward_field, diag_blocks,
                    precond, off_blocks, off_index.T,
                )
            )
        )
        lam, grad = pl.pallas_call(
            write_out,
            out_shape=(
                pltpu.HBM((sources, nodes), F32),
                pltpu.HBM((1, nodes // groups), F32),
            ),
            in_specs=[pl.BlockSpec(memory_space=pltpu.VMEM)] * 2,
            out_specs=(pl.BlockSpec(memory_space=pltpu.HBM),) * 2,
            scratch_shapes=[pltpu.SemaphoreType.DMA((2,))],
        )(
            pltpu.with_memory_space_constraint(lam, pltpu.VMEM),
            pltpu.with_memory_space_constraint(grad, pltpu.VMEM),
        )
        return lam, grad.reshape(nodes // groups)

    return jax.shard_map(
        shards,
        mesh=mesh,
        in_specs=(
            P("src", "space"),
            P("space"),
            P("src", "space"),
            P(None, "space"),
            P(None, "space"),
            P(None, None, "space"),
            P("space", None),
        ),
        out_specs=(P("src", "space"), P(("space", "src"))),
        check_vma=False,
    )
```

```python
import functools

import jax
import jax.numpy as jnp
from jax import lax
from jax.experimental import pallas as pl
from jax.experimental.pallas import tpu as pltpu
from jax.sharding import PartitionSpec as P

MESH = pl.DeviceIdType.MESH
F32 = jnp.float32
BF16 = jnp.bfloat16
NT = (((1,), (1,)), ((), ()))


def kernel(
    cfg,
    misfit_h, node_h, field_h, diag_h, cond_h, off_h, index_h,
    lam_out, grad_out,
    misfit_v, node_v, field_v, diag_v, cond_v, off_v, index_s,
    rhs_v, cond2_v, driven_v, tiles1, tiles2, tiles_f,
    stage, landed, grad_send, grad_recv,
    load_sem, halo_send, halo_recv, gsend_sem, grecv_sem, present,
):
    spaces, groups, pairs, rim, terms = cfg
    blocks = 2 * pairs
    ext = rim // 2
    inner = range(ext, pairs - ext)
    low = range(0, ext)
    high = range(pairs - ext, pairs)

    loads = []
    for at, (src, dst) in enumerate(
        [
            (misfit_h, misfit_v), (node_h, node_v), (cond_h, cond_v), (field_h, field_v),
            (index_h, index_s), (diag_h, diag_v), (off_h, off_v),
        ]
    ):
        loads.append(pltpu.make_async_copy(src, dst, load_sem.at[at]))
    misfit_l, node_l, cond_l, field_l, index_l, diag_l, off_l = loads

    me = lax.axis_index("space")
    group = lax.axis_index("src")
    down = lax.rem(me + spaces - 1, spaces)
    up = lax.rem(me + 1, spaces)
    barrier = pltpu.get_barrier_semaphore()
    has = (me > 0, me < spaces - 1)
    for side, neighbour in enumerate((down, up)):

        @pl.when(has[side])
        def _():
            pl.semaphore_signal(
                barrier, inc=1, device_id={"space": neighbour}, device_id_type=MESH
            )

    core = group + 1 - 2 * lax.rem(group, 2)
    across = group + 2 - 4 * lax.rem(lax.div(group, 2), 2)
    after = lax.rem(group + 4, groups)
    before = lax.rem(group + groups - 4, groups)
    for peer in (after, before, across, core):
        pl.semaphore_signal(barrier, inc=1, device_id={"src": peer}, device_id_type=MESH)
    for copy in loads:
        copy.start()

    left = lax.broadcasted_iota(jnp.int32, (8, 128), 1) < 64
    upper_rows = lax.broadcasted_iota(jnp.int32, (16, 128), 0) < 8
    zero = jnp.zeros((8, 128), F32)

    def lanes(pair):
        return pl.ds(pair * 128, 128)

    node_l.wait()
    misfit_l.wait()
    chunk = 256
    total = None
    for at in range(0, misfit_v.shape[1], chunk):
        node = node_v[:, pl.ds(at, chunk)]
        pair_of = jnp.broadcast_to(node // 128, (8, chunk))
        lane_of = jnp.broadcast_to(node % 128, (128, chunk))
        value = misfit_v[:, pl.ds(at, chunk)]
        coarse = value.astype(BF16).astype(F32)
        fine = value - coarse
        rows = []
        for pair in range(pairs):
            mask = pair_of == pair
            rows.append(jnp.where(mask, coarse, 0.0))
            rows.append(jnp.where(mask, fine, 0.0))
        spread = jnp.concatenate(rows, axis=0).astype(BF16)
        hot = lax.broadcasted_iota(jnp.int32, (128, chunk), 0) == lane_of
        hot = jnp.where(hot, 1.0, 0.0).astype(BF16)
        part = lax.dot_general(spread, hot, NT, preferred_element_type=F32)
        total = part if total is None else total + part
    rhs = [total[16 * p : 16 * p + 8] + total[16 * p + 8 : 16 * p + 16] for p in range(pairs)]

    def pick(y):
        return jnp.where(left, y[0:8], y[8:16])

    def smooth(pair, res):
        x = jnp.concatenate([jnp.where(left, res, zero), jnp.where(left, zero, res)], axis=0)
        w = cond_v[:, lanes(pair)]
        w = jnp.concatenate([w, w], axis=0)
        return pick(lax.dot_general(x.astype(BF16), w, NT, preferred_element_type=F32))

    def expand(tiles, first, v):
        swapped = pltpu.roll(v, 64, 1)
        tiles[first] = jnp.concatenate(
            [jnp.where(left, v, zero), jnp.where(left, zero, swapped)], axis=0
        ).astype(BF16)
        tiles[first + 1] = jnp.concatenate(
            [jnp.where(left, swapped, zero), jnp.where(left, zero, v)], axis=0
        ).astype(BF16)

    def apply(pair, tiles):
        parts = [jnp.where(upper_rows, tiles[rim + 2 * pair], tiles[rim + 2 * pair + 1])]
        weights = [diag_v[:, lanes(pair)]]
        for k in range(terms):
            parts.append(
                jnp.where(
                    upper_rows,
                    tiles[index_s[k, 2 * pair]],
                    tiles[index_s[k, 2 * pair + 1]],
                )
            )
            weights.append(off_v[k, :, lanes(pair)])
        x = jnp.concatenate(parts, axis=1)
        w = jnp.concatenate(weights, axis=1)
        return lax.dot_general(x, w, NT, preferred_element_type=F32)

    def stage_side(which, side, values):
        for at in range(0, ext, 2):
            stage[side, which, at // 2] = jnp.concatenate(
                [values[at], values[at + 1]], axis=0
            ).astype(BF16)

    def halo(which, side):
        return pltpu.make_async_remote_copy(
            src_ref=stage.at[side, which],
            dst_ref=landed.at[which, 1 - side],
            send_sem=halo_send.at[side],
            recv_sem=halo_recv.at[2 * which + 1 - side],
            device_id={"space": down if side == 0 else up},
            device_id_type=MESH,
        )

    def start(which, side):
        @pl.when(has[side])
        def _():
            halo(which, side).start()

    def receive(which, side, tiles):
        @pl.when(has[side])
        def _():
            halo(which, 1 - side).wait_recv()

        base = 0 if side == 0 else rim + blocks
        for at in range(0, ext, 2):
            both = landed[which, side, at // 2].astype(F32)
            both = jnp.where(has[side], both, 0.0)
            expand(tiles, base + 2 * at, both[0:8])
            expand(tiles, base + 2 * at + 2, both[8:16])

    cond_l.wait()
    lam = [None] * pairs
    for pair in high:
        lam[pair] = smooth(pair, rhs[pair])
    stage_side(0, 1, [lam[p] for p in high])
    pl.semaphore_wait(barrier, 4 + jnp.where(has[0], 1, 0) + jnp.where(has[1], 1, 0))
    start(0, 1)
    def tell(at, peer):
        pl.semaphore_signal(
            present.at[at], inc=1, device_id={"src": peer}, device_id_type=MESH
        )

    tell(0, after)
    for pair in low:
        lam[pair] = smooth(pair, rhs[pair])
    stage_side(0, 0, [lam[p] for p in low])
    start(0, 0)
    field_l.wait()
    field = [field_v[:, lanes(p)].astype(F32) for p in range(pairs)]

    for pair in inner:
        lam[pair] = smooth(pair, rhs[pair])
    for pair in range(pairs):
        expand(tiles1, rim + 2 * pair, lam[pair])
        expand(tiles_f, rim + 2 * pair, field[pair])

    for pair in range(pairs):
        rhs_v[pair] = jnp.concatenate([rhs[pair], pltpu.roll(rhs[pair], 64, 1)], axis=0)
        w = cond_v[:, lanes(pair)]
        cond2_v[pair] = jnp.concatenate([w[:, 0:64], w[:, 64:128]], axis=0)

    index_l.wait()
    diag_l.wait()
    off_l.wait()

    def sweep(some, tiles):
        products = [apply(pair, tiles) for pair in some]
        residues = [
            (rhs_v[pair, :, 0:64] - y).astype(BF16) for pair, y in zip(some, products)
        ]
        steps = [
            lax.dot_general(res, cond2_v[pair], NT, preferred_element_type=F32)
            for pair, res in zip(some, residues)
        ]
        for pair, step in zip(some, steps):
            lam[pair] = lam[pair] + pick(step)

    pl.semaphore_wait(present.at[0], 1)
    tell(1, across)
    sweep(inner, tiles1)
    for side, own in ((1, high), (0, low)):
        stage_side(2, side, [field[p] for p in own])
        start(2, side)
    pl.semaphore_wait(present.at[1], 1)
    tell(2, core)
    for side, own in ((1, high), (0, low)):
        receive(0, side, tiles1)
        sweep(own, tiles1)
        stage_side(1, side, [lam[p] for p in own])
        start(1, side)
    for pair in range(pairs):
        expand(tiles2, rim + 2 * pair, lam[pair])

    for side in (1, 0):
        receive(2, side, tiles_f)
    for pair in range(pairs):
        y = apply(pair, tiles_f)
        driven_v[pair] = jnp.concatenate([y[0:8], y[8:16]], axis=1)

    def send_row(pair):
        return pltpu.make_async_remote_copy(
            src_ref=grad_send.at[pair],
            dst_ref=grad_recv.at[group],
            send_sem=gsend_sem.at[0],
            recv_sem=grecv_sem.at[0],
            device_id={"src": pair},
            device_id_type=MESH,
        )

    def finish(some, first=False):
        sweep(some, tiles2)
        rows = [-jnp.sum(lam[p] * driven_v[p], axis=0, keepdims=True) for p in some]
        for pair, row in zip(some, rows):
            grad_send[pair] = row
            lam_out[:, lanes(pair)] = lam[pair]
        if first:
            pl.semaphore_wait(present.at[2], 1)
        for pair in some:

            @pl.when(group != pair)
            def _():
                send_row(pair).start()

    finish(inner, first=True)
    for side, own in ((0, low), (1, high)):
        receive(1, side, tiles2)
        finish(own)

    grad_recv[pl.ds(group, 1)] = grad_send[pl.ds(group, 1)]
    for side in (0, 1):

        @pl.when(has[side])
        def _():
            pltpu.make_async_copy(stage.at[side], stage.at[side], halo_send.at[side]).wait()

    others = pl.ds(0, groups - 1)
    for sem in (gsend_sem, grecv_sem):
        pltpu.make_async_copy(grad_send.at[others], grad_recv.at[others], sem.at[0]).wait()

    grad_out[...] = jnp.sum(grad_recv[...], axis=0)


def write_out(lam, grad, lam_out, grad_out, sem):
    copies = [
        pltpu.make_async_copy(lam, lam_out, sem.at[0]),
        pltpu.make_async_copy(grad, grad_out, sem.at[1]),
    ]
    for copy in copies:
        copy.start()
    for copy in copies:
        copy.wait()


def solution(mesh):
    spaces, groups = mesh.shape["space"], mesh.shape["src"]

    def shards(misfit, electrode_node, forward_field, diag_blocks, precond, off_blocks, off_index):
        sources, nodes = forward_field.shape
        width = diag_blocks.shape[0]
        blocks = nodes // width
        terms = off_blocks.shape[0]
        rim = 3 * blocks // 8
        pairs = blocks // 2
        electrodes = misfit.shape[1]
        ext_blocks = blocks + 2 * rim
        sent = rim // 4
        lam, grad = pl.pallas_call(
            functools.partial(kernel, (spaces, groups, pairs, rim, terms)),
            out_shape=(
                pltpu.VMEM((sources, nodes), F32),
                pltpu.VMEM((1, nodes // groups), F32),
            ),
            in_specs=[pl.BlockSpec(memory_space=pltpu.HBM)] * 7,
            out_specs=(pl.BlockSpec(memory_space=pltpu.VMEM), pl.BlockSpec(memory_space=pltpu.VMEM)),
            scratch_shapes=[
                pltpu.VMEM((sources, electrodes), F32),
                pltpu.VMEM((1, electrodes), jnp.int32),
                pltpu.VMEM((sources, nodes), BF16),
                pltpu.VMEM((width, nodes), BF16),
                pltpu.VMEM((width, nodes), BF16),
                pltpu.VMEM((terms, width, nodes), BF16),
                pltpu.SMEM((terms, blocks), jnp.int32),
                pltpu.VMEM((pairs, 16, 128), F32),
                pltpu.VMEM((pairs, 128, width), BF16),
                pltpu.VMEM((pairs, sources, 128), F32),
                pltpu.VMEM((ext_blocks, 16, 128), BF16),
                pltpu.VMEM((ext_blocks, 16, 128), BF16),
                pltpu.VMEM((ext_blocks, 16, 128), BF16),
                pltpu.VMEM((2, 3, sent, 16, 128), BF16),
                pltpu.VMEM((3, 2, sent, 16, 128), BF16),
                pltpu.VMEM((pairs, 1, 128), F32),
                pltpu.VMEM((groups, 1, 128), F32),
                pltpu.SemaphoreType.DMA((7,)),
                pltpu.SemaphoreType.DMA((2,)),
                pltpu.SemaphoreType.DMA((6,)),
                pltpu.SemaphoreType.DMA((1,)),
                pltpu.SemaphoreType.DMA((1,)),
                pltpu.SemaphoreType.REGULAR((3,)),
            ],
            compiler_params=pltpu.CompilerParams(
                collective_id=0, has_side_effects=True, vmem_limit_bytes=32 * 1024 * 1024
            ),
        )(
            *(
                pltpu.with_memory_space_constraint(operand, pltpu.HBM)
                for operand in (
                    misfit, electrode_node.reshape(1, electrodes), forward_field, diag_blocks,
                    precond, off_blocks, off_index.T,
                )
            )
        )
        lam, grad = pl.pallas_call(
            write_out,
            out_shape=(
                pltpu.HBM((sources, nodes), F32),
                pltpu.HBM((1, nodes // groups), F32),
            ),
            in_specs=[pl.BlockSpec(memory_space=pltpu.VMEM)] * 2,
            out_specs=(pl.BlockSpec(memory_space=pltpu.HBM),) * 2,
            scratch_shapes=[pltpu.SemaphoreType.DMA((2,))],
        )(
            pltpu.with_memory_space_constraint(lam, pltpu.VMEM),
            pltpu.with_memory_space_constraint(grad, pltpu.VMEM),
        )
        return lam, grad.reshape(nodes // groups)

    return jax.shard_map(
        shards,
        mesh=mesh,
        in_specs=(
            P("src", "space"),
            P("space"),
            P("src", "space"),
            P(None, "space"),
            P(None, "space"),
            P(None, None, "space"),
            P("space", None),
        ),
        out_specs=(P("src", "space"), P(("space", "src"))),
        check_vma=False,
    )
```
